256 devices in a mesh: seq: 64 (over z, x, y_lo), head: 4 (over y_hi, core).
Axes of the slice: x: 4, y: 4 (y_hi: 2, y_lo: 2; y = y_hi * 2 + y_lo), z: 8, core: 2. Of those that a mesh axis runs over, the one named last changes fastest.
Arguments:
- queries: bfloat16 [16384, 512], P('seq', 'head'), may hold values from -32 to 32
- keys: bfloat16 [16384, 512], P('seq', 'head'), may hold values from -32 to 32
- values: bfloat16 [16384, 512], P('seq', 'head'), may hold values from -6 to 6
- d_out: bfloat16 [16384, 512], P('seq', 'head'), may hold values from -6 to 6
Outputs:
- d_queries: bfloat16 [16384, 512], P('seq')
- d_keys: bfloat16 [16384, 512], P('seq')
- d_values: bfloat16 [16384, 512], P('seq')
The draws below stay inside these ranges and needn't reach their ends.
All inputs are finite; a program needn't handle non-finite values.
Results may differ from the reference program's by a relative error of at most 0.008.
Values may be sent and summed in bfloat16 or wider, within the bound.
A program may use at most 128 MiB of HBM per device.

```python
import jax
import jax.numpy as jnp
from jax import lax

HEAD_DIM = 128
HEADS = 4
TOKENS = 16384
FEATURES = 512


def draw_queries(key, part):
    key = jax.random.fold_in(key, 1)
    result = 1.5 * jax.random.normal(key, (TOKENS, HEADS * HEAD_DIM), jnp.float32)
    return jnp.clip(result, -32.0, 32.0).astype(jnp.bfloat16)


def draw_keys(key, part):
    key = jax.random.fold_in(key, 2)
    result = jax.random.normal(key, (TOKENS, HEADS * HEAD_DIM), jnp.float32)
    return jnp.clip(result, -32.0, 32.0).astype(jnp.bfloat16)


def steps_of(own_key, dims, shards, low, top_value):
    def one(position, shards_of):
        draws = jax.random.uniform(jax.random.fold_in(jax.random.fold_in(own_key, 6), position), (shards_of,), jnp.float32, low / len(shards), top_value / len(shards))
        return jnp.repeat(jnp.exp(draws), dims[position] // shards_of).reshape((-1,) + (1,) * (len(dims) - position - 1))

    level = one(*shards[0])
    for cut in shards[1:]:
        level = level * one(*cut)
    return level


def scatter_about(key, extent, scale, bound, cuts=(), kind=jnp.bfloat16):
    drawn = scale * jax.random.normal(key, extent, jnp.float32)
    if cuts:
        drawn = drawn * steps_of(key, extent, cuts, -0.22, 0.18)
    return jnp.clip(drawn, -bound, bound).astype(kind)


def setup_inputs(seed: int = 0) -> dict:
    splits = jax.random.split(jax.random.key(seed), 5)
    return {
        "queries": draw_queries(jax.random.fold_in(splits[4], 71), 0),
        "keys": draw_keys(jax.random.fold_in(splits[4], 71), 0),
        "values": scatter_about(splits[2], (TOKENS, FEATURES), 1.0, 6.0, ((0, 64), (1, 4))),
        "d_out": scatter_about(splits[3], (TOKENS, FEATURES), 1.0, 6.0, ((0, 64), (1, 4))),
    }


def one_head(items):
    query, key, value, cot = items
    scale = HEAD_DIM ** -0.5
    scores = jnp.dot(query, key.T, preferred_element_type=jnp.float32) * scale
    top = jnp.max(scores, axis=1)
    lse = top + jnp.log(jnp.sum(jnp.exp(scores - top[:, None]), axis=1))
    probs = jnp.exp(scores - lse[:, None])
    d_probs = jnp.dot(cot, value.T, preferred_element_type=jnp.float32)
    delta = jnp.sum(probs * d_probs, axis=1)
    d_scores = probs * (d_probs - delta[:, None])
    probs_low = probs.astype(jnp.bfloat16)
    d_low = d_scores.astype(jnp.bfloat16)
    d_value = jnp.dot(probs_low.T, cot, preferred_element_type=jnp.float32)
    d_query = jnp.dot(d_low, key, preferred_element_type=jnp.float32) * scale
    d_key = jnp.dot(d_low.T, query, preferred_element_type=jnp.float32) * scale
    return d_query.astype(jnp.bfloat16), d_key.astype(jnp.bfloat16), d_value.astype(jnp.bfloat16)


def split_heads(array):
    return array.reshape(TOKENS, HEADS, HEAD_DIM).transpose(1, 0, 2)


def join_heads(array):
    return array.transpose(1, 0, 2).reshape(TOKENS, HEADS * HEAD_DIM)


def reference(queries, keys, values, d_out):
    d_query, d_key, d_value = lax.map(one_head, (split_heads(queries), split_heads(keys), split_heads(values), split_heads(d_out)))
    return join_heads(d_query), join_heads(d_key), join_heads(d_value)
```

```python
import math

import jax
import jax.numpy as jnp
from jax import lax
from jax.experimental import pallas as pl
from jax.experimental.pallas import tpu as pltpu
from jax.sharding import PartitionSpec as P

HEAD_DIM = 128
NZ, NX, NY = 8, 4, 2
NXY = NX * NY
NCORE = 2
SCALE = 1.0 / math.sqrt(HEAD_DIM)
LOG2E_SCALE = math.log2(math.e) * SCALE
MESH = pl.DeviceIdType.MESH
F32 = jnp.float32
BF16 = jnp.bfloat16
NT = (((1,), (1,)), ((), ()))
NN = (((1,), (0,)), ((), ()))


def dot(a, b, dims):
    return lax.dot_general(a, b, dims, preferred_element_type=F32)


Z_AT = [0, 1, -1, 2, -2, 3, -3, 4]
XY_AT = [(0, 0), (0, 1), (1, 0), (-1, 0), (1, 1), (-1, 1), (2, 0), (2, 1)]


def kernel(
    q_in,
    k_in,
    v_in,
    do_in,
    oq,
    ok,
    ov,
    qd,
    kv,
    scores,
    dprobs,
    top,
    mass,
    weighted,
    st_own,
    st_all,
    lse,
    delta,
    dqt,
    pkv,
    send_anti,
    recv_anti,
    send_one,
    recv_one,
    send_y,
    recv_y,
    zsend,
    zrecv4,
    zrecv,
    fin,
    local_sem,
    send_sem,
    recv_sem,
):
    rows = q_in.shape[0]
    total_q = NZ * rows
    total_k = NXY * rows
    seq = lax.axis_index("seq")
    head = lax.axis_index("head")
    z = seq // NXY
    x = (seq // NY) % NX
    y = seq % NY

    def at(dz=0, dx=0, dy=0):
        zz = (z + dz + NZ) % NZ
        xx = (x + dx + NX) % NX
        yy = (y + dy) % NY
        return (zz * NXY + xx * NY + yy, head)

    def head_at(dh):
        return (seq, (head + dh) % (2 * NCORE))

    counter = [0]
    sent = []

    def remote(src, dst, device):
        i = counter[0]
        counter[0] += 1
        c = pltpu.make_async_remote_copy(
            src_ref=src,
            dst_ref=dst,
            send_sem=send_sem.at[i],
            recv_sem=recv_sem.at[i],
            device_id=device,
            device_id_type=MESH,
        )
        sent.append(c)
        return c

    own = [
        pltpu.make_async_copy(src, dst, local_sem.at[i])
        for i, (src, dst) in enumerate(
            [
                (q_in, qd.at[0, 0]),
                (do_in, qd.at[1, 0]),
                (k_in, kv.at[0, 0]),
                (v_in, kv.at[1, 0]),
            ]
        )
    ]
    for c in own:
        c.start()

    barrier = pltpu.get_barrier_semaphore()
    peers = [at(dz=d) for d in range(1, NZ)]
    peers += [at(dx=1), at(dx=-1), at(dy=1)]
    peers += [head_at(d) for d in range(1, 2 * NCORE)]
    for p in peers:
        pl.semaphore_signal(barrier, inc=1, device_id=p, device_id_type=MESH)
    for c in own:
        c.wait()
    pl.semaphore_wait(barrier, len(peers))

    zc = {}
    for part in range(2):
        zc[2, part] = remote(qd.at[part, 0], qd.at[part, 2], at(dz=1))
        zc[1, part] = remote(qd.at[part, 0], qd.at[part, 1], at(dz=-1))
    kc = {}
    for part in range(2):
        kc[3, part] = remote(kv.at[part, 0], kv.at[part, 3], at(dx=1))
        kc[2, part] = remote(kv.at[part, 0], kv.at[part, 2], at(dx=-1))
        kc[1, part] = remote(kv.at[part, 0], kv.at[part, 1], at(dy=1))
    for part in range(2):
        for c in (zc[2, part], zc[1, part], kc[3, part], kc[2, part], kc[1, part]):
            c.start()

    def z_forward(a, part):
        zc[a, part].wait_recv()
        b = a + 2
        if b < 7:
            zc[b, part] = remote(
                qd.at[part, a], qd.at[part, b], at(dz=-1 if a % 2 else 1)
            )
            zc[b, part].start()
        elif (a == 6) == (part == 0):
            zc[7, part] = remote(
                qd.at[part, a], qd.at[part, 7], at(dz=-1 if a % 2 else 1)
            )
            zc[7, part].start()

    for part in range(2):
        z_forward(2, part)
        z_forward(1, part)
        kc[1, part].wait_recv()
        kc[5, part] = remote(kv.at[part, 1], kv.at[part, 5], at(dx=1))
        kc[4, part] = remote(kv.at[part, 1], kv.at[part, 4], at(dx=-1))
        kc[5, part].start()
        kc[4, part].start()
        kc[3, part].wait_recv()
        kc[2, part].wait_recv()
        if part == 0:
            kc[6, 0] = remote(kv.at[0, 3], kv.at[0, 6], at(dx=1))
            kc[6, 0].start()
        else:
            kc[6, 1] = remote(kv.at[1, 2], kv.at[1, 6], at(dx=-1))
            kc[6, 1].start()
    for part in range(2):
        z_forward(4, part)
        z_forward(3, part)
    for part in range(2):
        kc[6, part].wait_recv()
        kc[7, part] = remote(kv.at[part, 6], kv.at[part, 7], at(dy=1))
        kc[7, part].start()
    for part in range(2):
        z_forward(6, part)
        z_forward(5, part)
    for part in range(2):
        kc[5, part].wait_recv()
        kc[4, part].wait_recv()
    for part in range(2):
        kc[7, part].wait_recv()
    for part in range(2):
        zc[7, part].wait_recv()

    qb = 2 * rows

    @pl.loop(0, NZ // 2)
    def _(i):
        qs = pl.ds(pl.multiple_of(i * qb, qb), qb)
        two = pl.ds(pl.multiple_of(i * 2, 2), 2)
        qq = qd[0, two].reshape(qb, HEAD_DIM)
        dd = qd[1, two].reshape(qb, HEAD_DIM)
        s = dot(kv[0].reshape(total_k, HEAD_DIM), qq, NT)
        scores[:, qs] = s
        m = jnp.max(s, axis=0, keepdims=True) * LOG2E_SCALE
        e = jnp.exp2(s * LOG2E_SCALE - m)
        dp = dot(kv[1].reshape(total_k, HEAD_DIM), dd, NT)
        dprobs[:, qs] = dp
        l = jnp.sum(e, axis=0, keepdims=True)
        w = jnp.sum(e * dp, axis=0, keepdims=True)
        top[:, qs] = m + jnp.log2(l)
        weighted[:, qs] = w / l

    for slot, dz in enumerate(Z_AT):
        o = (z + dz + NZ) % NZ
        st_own[0, pl.ds(o, 1), :] = top[:, pl.ds(slot * rows, rows)]
        st_own[1, pl.ds(o, 1), :] = weighted[:, pl.ds(slot * rows, rows)]
    sc = []
    for d in range(1, NZ):
        c = remote(st_own, st_all.at[d], at(dz=d))
        c.start()
        sc.append(c)
    st_all[0] = st_own[...]
    for c in sc:
        c.wait_recv()
    big = st_all[0, 0]
    for d in range(1, NZ):
        big = jnp.maximum(big, st_all[d, 0])
    mass_all = jnp.zeros_like(big)
    weighted_all = jnp.zeros_like(big)
    for d in range(NZ):
        f = jnp.exp2(st_all[d, 0] - big)
        mass_all += f
        weighted_all += f * st_all[d, 1]
    for c in sc:
        c.wait_send()
    st_own[0] = big + jnp.log2(mass_all)
    st_own[1] = weighted_all / mass_all
    for slot, dz in enumerate(Z_AT):
        o = (z + dz + NZ) % NZ
        lse[:, pl.ds(slot * rows, rows)] = st_own[0, pl.ds(o, 1), :]
        delta[:, pl.ds(slot * rows, rows)] = st_own[1, pl.ds(o, 1), :]

    dqt[...] = jnp.zeros(dqt.shape, F32)
    anti = {}
    for dy in range(2):
        anti[0, dy] = remote(send_anti.at[0, dy], recv_anti.at[0, dy], at(dx=1))
        anti[1, dy] = remote(send_anti.at[1, dy], recv_anti.at[1, dy], at(dx=-1))
    one = {}
    for dy in range(2):
        one[0, dy] = remote(send_one.at[0, dy], recv_one.at[0, dy], at(dx=1))
        one[1, dy] = remote(send_one.at[1, dy], recv_one.at[1, dy], at(dx=-1))
    ycopy = remote(send_y, recv_y, at(dy=1))

    @pl.loop(0, NXY)
    def _(it):
        slot = NXY - 1 - it
        ks = pl.ds(pl.multiple_of(slot * rows, rows), rows)
        kk = kv[0, slot]
        p = jnp.exp2(scores[ks, :] * LOG2E_SCALE - lse[...])
        ds = (p * (dprobs[ks, :] - delta[...])).astype(BF16)
        pkv[1] = dot(p.astype(BF16), qd[1].reshape(total_q, HEAD_DIM), NN)
        pkv[0] = dot(ds, qd[0].reshape(total_q, HEAD_DIM), NN) * SCALE
        dqt[...] += dot(kk.T, ds, NN)

        for dy in range(2):

            @pl.when(slot == 6 + dy)
            def _():
                for part in range(2):
                    send_anti[part, dy] = pkv[part].astype(BF16)
                    anti[part, dy].start()

            for side in range(2):

                @pl.when(slot == 2 + 2 * dy + side)
                def _():
                    anti[side, dy].wait_recv()
                    send_one[side, dy, side] = (
                        pkv[side] + recv_anti[side, dy].astype(F32)
                    ).astype(BF16)
                    send_one[side, dy, 1 - side] = pkv[1 - side].astype(BF16)
                    one[side, dy].start()

        @pl.when(slot == 1)
        def _():
            one[0, 1].wait_recv()
            one[1, 1].wait_recv()
            for part in range(2):
                send_y[part] = (
                    pkv[part]
                    + recv_one[0, 1, part].astype(F32)
                    + recv_one[1, 1, part].astype(F32)
                ).astype(BF16)
            ycopy.start()

    half = rows // 2

    def mine(slot):
        return dqt[:, pl.ds(slot * rows, rows)].T * SCALE

    t = mine(7)
    zsend[0, 0] = t.astype(BF16)
    far = [
        remote(zsend.at[0, 0, pl.ds(0, half)], zrecv4.at[0], at(dz=1)),
        remote(zsend.at[0, 0, pl.ds(half, half)], zrecv4.at[1], at(dz=-1)),
    ]
    for c in far:
        c.start()
    before = None
    for hop in range(3):
        now = []
        for side in range(2):
            own_part = mine(5 - 2 * hop + side)
            if hop == 0:
                far[side].wait_recv()
                lo = own_part[:half]
                hi = own_part[half:]
                if side == 0:
                    lo = lo + zrecv4[0].astype(F32)
                else:
                    hi = hi + zrecv4[1].astype(F32)
                zsend[side, 1, pl.ds(0, half)] = lo.astype(BF16)
                zsend[side, 1, pl.ds(half, half)] = hi.astype(BF16)
            else:
                before[side].wait_recv()
                zsend[side, 1 + hop] = (
                    own_part + zrecv[side, hop - 1].astype(F32)
                ).astype(BF16)
            c = remote(
                zsend.at[side, 1 + hop], zrecv.at[side, hop], at(dz=1 - 2 * side)
            )
            c.start()
            now.append(c)
        before = now

    def finish(index, out):
        cols = pl.ds(pl.multiple_of(head * HEAD_DIM, HEAD_DIM), HEAD_DIM)
        cs = [
            remote(fin.at[index], out.at[:, cols], head_at(d))
            for d in range(1, 2 * NCORE)
        ]
        c0 = pltpu.make_async_copy(fin.at[index], out.at[:, cols], local_sem.at[index])
        for c in cs:
            c.start()
        c0.start()
        return c0, cs

    one[0, 0].wait_recv()
    one[1, 0].wait_recv()
    ycopy.wait_recv()
    ends = []
    for part, out in ((0, ok), (1, ov)):
        fin[part] = (
            pkv[part]
            + recv_one[0, 0, part].astype(F32)
            + recv_one[1, 0, part].astype(F32)
            + recv_y[part].astype(F32)
        ).astype(BF16)
        ends.append(finish(part, out))
    own_part = mine(0)
    for side in range(2):
        before[side].wait_recv()
    fin[2] = (
        own_part + zrecv[0, 2].astype(F32) + zrecv[1, 2].astype(F32)
    ).astype(BF16)
    ends.append(finish(2, oq))
    for c0, cs in ends:
        c0.wait()
        for c in cs:
            c.wait_recv()
    for c in sent:
        if not any(c is s for s in sc):
            c.wait_send()


def local(queries, keys, values, d_out):
    rows, width = queries.shape
    total = NZ * rows
    any_spec = pl.BlockSpec(memory_space=pl.ANY)
    out = jax.ShapeDtypeStruct((rows, 2 * NCORE * width), BF16)
    vm = pltpu.VMEM
    return pl.pallas_call(
        kernel,
        out_shape=[out, out, out],
        in_specs=[any_spec] * 4,
        out_specs=[any_spec] * 3,
        scratch_shapes=[
            vm((2, NZ, rows, width), BF16),
            vm((2, NXY, rows, width), BF16),
            vm((total, total), F32),
            vm((total, total), F32),
            vm((1, total), F32),
            vm((1, total), F32),
            vm((1, total), F32),
            vm((2, NZ, rows), F32),
            vm((NZ, 2, NZ, rows), F32),
            vm((1, total), F32),
            vm((1, total), F32),
            vm((width, total), F32),
            vm((2, rows, width), F32),
            vm((2, 2, rows, width), BF16),
            vm((2, 2, rows, width), BF16),
            vm((2, 2, 2, rows, width), BF16),
            vm((2, 2, 2, rows, width), BF16),
            vm((2, rows, width), BF16),
            vm((2, rows, width), BF16),
            vm((2, 4, rows, width), BF16),
            vm((2, rows // 2, width), BF16),
            vm((2, 3, rows, width), BF16),
            vm((3, rows, width), BF16),
            pltpu.SemaphoreType.DMA((4,)),
            pltpu.SemaphoreType.DMA((72,)),
            pltpu.SemaphoreType.DMA((72,)),
        ],
        compiler_params=pltpu.CompilerParams(
            collective_id=0, has_side_effects=True, vmem_limit_bytes=58 * 2**20
        ),
        name="attention_backward",
    )(queries, keys, values, d_out)


def solution(mesh):
    in_specs = (P("seq", "head"), P("seq", "head"), P("seq", "head"), P("seq", "head"))
    out_specs = (P("seq", None), P("seq", None), P("seq", None))
    return jax.shard_map(local, mesh=mesh, in_specs=in_specs, out_specs=out_specs, check_vma=False)
```

```python
import math

import jax
import jax.numpy as jnp
from jax import lax
from jax.experimental import pallas as pl
from jax.experimental.pallas import tpu as pltpu
from jax.sharding import PartitionSpec as P

HEAD_DIM = 128
NZ, NX, NY = 8, 4, 2
NXY = NX * NY
NCORE = 2
SCALE = 1.0 / math.sqrt(HEAD_DIM)
LOG2E_SCALE = math.log2(math.e) * SCALE
MESH = pl.DeviceIdType.MESH
F32 = jnp.float32
BF16 = jnp.bfloat16
NT = (((1,), (1,)), ((), ()))
NN = (((1,), (0,)), ((), ()))


def dot(a, b, dims):
    return lax.dot_general(a, b, dims, preferred_element_type=F32)


Z_AT = [0, 1, -1, 2, -2, 3, -3, 4]
XY_AT = [(0, 0), (0, 1), (1, 0), (-1, 0), (1, 1), (-1, 1), (2, 0), (2, 1)]


def kernel(
    q_in,
    k_in,
    v_in,
    do_in,
    oq,
    ok,
    ov,
    qd,
    kv,
    scores,
    dprobs,
    probs_low,
    d_low,
    kt,
    qdf,
    st_own,
    st_all,
    lse,
    delta,
    factor,
    pkv,
    dq_own,
    xsend,
    xrecv,
    zsend,
    zrecv,
    ysum,
    yrecv,
    fin,
    fin_q,
    local_sem,
    send_sem,
    recv_sem,
):
    rows = q_in.shape[0]
    total_q = NZ * rows
    total_k = NXY * rows
    seq = lax.axis_index("seq")
    head = lax.axis_index("head")
    z = seq // NXY
    x = (seq // NY) % NX
    y = seq % NY

    def at(dz=0, dx=0, dy=0):
        zz = (z + dz + NZ) % NZ
        xx = (x + dx + NX) % NX
        yy = (y + dy) % NY
        return (zz * NXY + xx * NY + yy, head)

    def head_at(dh):
        return (seq, (head + dh) % (2 * NCORE))

    counter = [0]
    sent = []

    def remote(src, dst, device):
        i = counter[0]
        counter[0] += 1
        c = pltpu.make_async_remote_copy(
            src_ref=src,
            dst_ref=dst,
            send_sem=send_sem.at[i],
            recv_sem=recv_sem.at[i],
            device_id=device,
            device_id_type=MESH,
        )
        sent.append(c)
        return c

    own = [
        pltpu.make_async_copy(src, dst, local_sem.at[i])
        for i, (src, dst) in enumerate(
            [
                (q_in, qd.at[0, 0]),
                (do_in, qd.at[1, 0]),
                (k_in, kv.at[0, 0]),
                (v_in, kv.at[1, 0]),
            ]
        )
    ]
    for c in own:
        c.start()

    barrier = pltpu.get_barrier_semaphore()
    peers = [at(dz=d) for d in range(1, NZ)]
    peers += [at(dx=1), at(dx=-1), at(dy=1)]
    peers += [head_at(d) for d in range(1, 2 * NCORE)]
    for p in peers:
        pl.semaphore_signal(barrier, inc=1, device_id=p, device_id_type=MESH)
    for c in own:
        c.wait()
    pl.semaphore_wait(barrier, len(peers))

    zc = {}
    for part in range(2):
        zc[2, part] = remote(qd.at[part, 0], qd.at[part, 2], at(dz=1))
        zc[1, part] = remote(qd.at[part, 0], qd.at[part, 1], at(dz=-1))
    kc = {}
    for part in range(2):
        kc[3, part] = remote(kv.at[part, 0], kv.at[part, 3], at(dx=1))
        kc[2, part] = remote(kv.at[part, 0], kv.at[part, 2], at(dx=-1))
        kc[1, part] = remote(kv.at[part, 0], kv.at[part, 1], at(dy=1))
    for part in range(2):
        for c in (zc[2, part], zc[1, part], kc[3, part], kc[2, part], kc[1, part]):
            c.start()

    def z_forward(a, part):
        zc[a, part].wait_recv()
        b = a + 2
        if b < 7:
            zc[b, part] = remote(
                qd.at[part, a], qd.at[part, b], at(dz=-1 if a % 2 else 1)
            )
            zc[b, part].start()
        elif (a == 6) == (part == 0):
            zc[7, part] = remote(
                qd.at[part, a], qd.at[part, 7], at(dz=-1 if a % 2 else 1)
            )
            zc[7, part].start()

    for part in range(2):
        z_forward(2, part)
        z_forward(1, part)
        kc[1, part].wait_recv()
        kc[5, part] = remote(kv.at[part, 1], kv.at[part, 5], at(dx=1))
        kc[4, part] = remote(kv.at[part, 1], kv.at[part, 4], at(dx=-1))
        kc[5, part].start()
        kc[4, part].start()
        kc[3, part].wait_recv()
        kc[2, part].wait_recv()
        if part == 0:
            kc[6, 0] = remote(kv.at[0, 3], kv.at[0, 6], at(dx=1))
            kc[6, 0].start()
        else:
            kc[6, 1] = remote(kv.at[1, 2], kv.at[1, 6], at(dx=-1))
            kc[6, 1].start()
    for part in range(2):
        z_forward(4, part)
        z_forward(3, part)
    for part in range(2):
        kc[6, part].wait_recv()
        kc[7, part] = remote(kv.at[part, 6], kv.at[part, 7], at(dy=1))
        kc[7, part].start()
    for part in range(2):
        z_forward(6, part)
        z_forward(5, part)
    for part in range(2):
        kc[5, part].wait_recv()
        kc[4, part].wait_recv()
    for part in range(2):
        kc[7, part].wait_recv()
    for part in range(2):
        zc[7, part].wait_recv()

    qb = 2 * rows
    nq = NZ // 2
    st_base = counter[0]
    counter[0] += nq * (NZ - 1)

    def stat_copy(i, d):
        k = st_base + i * (NZ - 1) + d - 1
        return pltpu.make_async_remote_copy(
            src_ref=st_own.at[i],
            dst_ref=st_all.at[d, i],
            send_sem=send_sem.at[k],
            recv_sem=recv_sem.at[k],
            device_id=at(dz=d),
            device_id_type=MESH,
        )

    @pl.loop(0, nq)
    def _(i):
        qs = pl.ds(pl.multiple_of(i * qb, qb), qb)
        two = pl.ds(pl.multiple_of(i * 2, 2), 2)
        qq = qd[0, two].reshape(qb, HEAD_DIM)
        dd = qd[1, two].reshape(qb, HEAD_DIM)
        s = dot(kv[0].reshape(total_k, HEAD_DIM), qq, NT)
        scores[:, qs] = s
        m = jnp.max(s, axis=0, keepdims=True) * LOG2E_SCALE
        e = jnp.exp2(s * LOG2E_SCALE - m)
        dp = dot(kv[1].reshape(total_k, HEAD_DIM), dd, NT)
        dprobs[:, qs] = dp
        l = jnp.sum(e, axis=0, keepdims=True)
        w = jnp.sum(e * dp, axis=0, keepdims=True)
        top = m + jnp.log2(l)
        w = w / l
        lse[:, qs] = top
        for r in range(4):
            st_own[i, pl.ds(r, 1), :] = top[:, r * 128 : (r + 1) * 128]
            st_own[i, pl.ds(4 + r, 1), :] = w[:, r * 128 : (r + 1) * 128]
        for d in range(1, NZ):
            stat_copy(i, d).start()

    for j in range(NXY):
        kt[:, pl.ds(j * rows, rows)] = kv[0, j].T

    @pl.loop(0, NXY)
    def _(j):
        ks = pl.ds(pl.multiple_of(j * rows, rows), rows)
        p = jnp.exp2(scores[ks, :] * LOG2E_SCALE - lse[...])
        scores[ks, :] = p
        probs_low[ks, :] = p.astype(BF16)

    st_all[0] = st_own[...]
    for i in range(nq):
        for d in range(1, NZ):
            stat_copy(i, d).wait_recv()
    for slot, dz in enumerate(Z_AT):
        tops, deltas = [], []
        for d in range(NZ):
            there = Z_AT.index((dz + d + 3) % NZ - 3)
            i, b = there // 2, there % 2
            tops.append(st_all[d, i, pl.ds(2 * b, 2), :])
            deltas.append(st_all[d, i, pl.ds(4 + 2 * b, 2), :])
        big = tops[0]
        for t in tops[1:]:
            big = jnp.maximum(big, t)
        mass = jnp.zeros_like(big)
        weighted = jnp.zeros_like(big)
        for t, w in zip(tops, deltas):
            f = jnp.exp2(t - big)
            mass += f
            weighted += f * w
        weighted = weighted / mass
        own_factor = jnp.exp2(tops[0] - (big + jnp.log2(mass)))
        for r in range(2):
            cols = pl.ds(slot * rows + r * 128, 128)
            delta[:, cols] = weighted[r : r + 1, :]
            factor[:, cols] = own_factor[r : r + 1, :]
        wide = jnp.broadcast_to(
            factor[:, pl.ds(slot * rows, rows)], (HEAD_DIM, rows)
        ).T
        for part in range(2):
            qdf[part, slot] = (qd[part, slot].astype(F32) * wide).astype(BF16)

    xc = {}
    for part in (1, 0):
        for slot in range(2, NXY):
            dx, dy = XY_AT[slot]
            xc[part, slot] = remote(
                xsend.at[part, slot], xrecv.at[part, slot], at(dx=dx)
            )
    zc2 = {
        slot: remote(zsend.at[slot], zrecv.at[slot], at(dz=Z_AT[slot]))
        for slot in range(1, NZ)
    }

    def key_side(part, left):
        @pl.loop(0, NXY)
        def _(it):
            slot = NXY - 1 - it
            ks = pl.ds(pl.multiple_of(slot * rows, rows), rows)
            t = dot(left[ks, :], qdf[part].reshape(total_q, HEAD_DIM), NN)
            if part == 0:
                t = t * SCALE
            xsend[part, slot] = t.astype(BF16)

            @pl.when(slot < 2)
            def _():
                pkv[part, jnp.minimum(slot, 1)] = t

            for s in range(2, NXY):

                @pl.when(slot == s)
                def _():
                    xc[part, s].start()

    key_side(1, probs_low)

    @pl.loop(0, nq)
    def _(it):
        i = nq - 1 - it
        qs = pl.ds(pl.multiple_of(i * qb, qb), qb)
        ds = (scores[:, qs] * (dprobs[:, qs] - delta[:, qs])).astype(BF16)
        d_low[:, qs] = ds
        t = dot(kt[...], ds, NN) * (factor[:, qs] * SCALE)
        for b in range(2):
            mine = t[:, b * rows : (b + 1) * rows].T
            zsend[i * 2 + b] = mine.astype(BF16)

            @pl.when(i * 2 + b == 0)
            def _():
                dq_own[...] = mine

        for s in range(NZ):
            if s:

                @pl.when(i == s // 2)
                def _():
                    zc2[s].start()

    key_side(0, d_low)

    def up(ref):
        return ref.astype(F32)

    yc = {}

    def over_x(part):
        for dy in (1, 0):
            total = pkv[part, dy]
            for slot in range(2, NXY):
                if XY_AT[slot][1] == dy:
                    xc[part, slot].wait_recv()
                    total += up(xrecv[part, slot])
            ysum[part, dy] = total.astype(BF16)
            seq_to, _ = at(dy=dy)
            far = (head + NCORE) % (2 * NCORE)
            if dy:
                yc[part, 0] = remote(
                    ysum.at[part, 1], yrecv.at[part, 0], (seq_to, head)
                )
                yc[part, 0].start()
            yc[part, 1 + dy] = remote(
                ysum.at[part, dy], yrecv.at[part, 1 + dy], (seq_to, far)
            )
            yc[part, 1 + dy].start()

    def columns(out, h):
        return out.at[
            :, pl.ds(pl.multiple_of(h * HEAD_DIM, HEAD_DIM), HEAD_DIM)
        ]

    ends = []
    other = head + 1 - 2 * (head % 2)

    def over_y(part, out):
        yc[part, 0].wait_recv()
        fin[part, 0] = (up(ysum[part, 0]) + up(yrecv[part, 0])).astype(BF16)
        yc[part, 1].wait_recv()
        yc[part, 2].wait_recv()
        fin[part, 1] = (up(yrecv[part, 1]) + up(yrecv[part, 2])).astype(BF16)
        for b in range(2):
            cols = columns(out, (head + NCORE * b) % (2 * NCORE))
            c = remote(fin.at[part, b], cols, (seq, other))
            c.start()
            ends.append(c.wait_recv)
            c = pltpu.make_async_copy(fin.at[part, b], cols, local_sem.at[2 * part + b])
            c.start()
            ends.append(c.wait)

    over_x(1)
    over_x(0)
    over_y(1, ov)
    total = dq_own[...]
    for slot in range(1, NZ):
        zc2[slot].wait_recv()
        total += up(zrecv[slot])
    fin_q[...] = total.astype(BF16)
    cols = columns(oq, head)
    for d in range(1, 2 * NCORE):
        c = remote(fin_q, cols, head_at(d))
        c.start()
        ends.append(c.wait_recv)
    c = pltpu.make_async_copy(fin_q, cols, local_sem.at[4])
    c.start()
    ends.append(c.wait)
    over_y(0, ok)
    for wait in ends:
        wait()
    for c in sent:
        c.wait_send()
    for i in range(nq):
        for d in range(1, NZ):
            stat_copy(i, d).wait_send()


def local(queries, keys, values, d_out):
    rows, width = queries.shape
    total = NZ * rows
    any_spec = pl.BlockSpec(memory_space=pl.ANY)
    out = jax.ShapeDtypeStruct((rows, 2 * NCORE * width), BF16)
    vm = pltpu.VMEM
    return pl.pallas_call(
        kernel,
        out_shape=[out, out, out],
        in_specs=[any_spec] * 4,
        out_specs=[any_spec] * 3,
        scratch_shapes=[
            vm((2, NZ, rows, width), BF16),
            vm((2, NXY, rows, width), BF16),
            vm((total, total), F32),
            vm((total, total), F32),
            vm((total, total), BF16),
            vm((total, total), BF16),
            vm((width, total), BF16),
            vm((2, NZ, rows, width), BF16),
            vm((NZ // 2, 8, 128), F32),
            vm((NZ, NZ // 2, 8, 128), F32),
            vm((1, total), F32),
            vm((1, total), F32),
            vm((1, total), F32),
            vm((2, 2, rows, width), F32),
            vm((rows, width), F32),
            vm((2, NXY, rows, width), BF16),
            vm((2, NXY, rows, width), BF16),
            vm((NZ, rows, width), BF16),
            vm((NZ, rows, width), BF16),
            vm((2, 2, rows, width), BF16),
            vm((2, 3, rows, width), BF16),
            vm((2, 2, rows, width), BF16),
            vm((rows, width), BF16),
            pltpu.SemaphoreType.DMA((5,)),
            pltpu.SemaphoreType.DMA((112,)),
            pltpu.SemaphoreType.DMA((112,)),
        ],
        compiler_params=pltpu.CompilerParams(
            collective_id=0, has_side_effects=True, vmem_limit_bytes=62 * 2**20
        ),
        name="attention_backward",
    )(queries, keys, values, d_out)


def solution(mesh):
    in_specs = (P("seq", "head"), P("seq", "head"), P("seq", "head"), P("seq", "head"))
    out_specs = (P("seq", None), P("seq", None), P("seq", None))
    return jax.shard_map(local, mesh=mesh, in_specs=in_specs, out_specs=out_specs, check_vma=False)
```

```python
import math

import jax
import jax.numpy as jnp
from jax import lax
from jax.experimental import pallas as pl
from jax.experimental.pallas import tpu as pltpu
from jax.sharding import PartitionSpec as P

HEAD_DIM = 128
NZ, NX, NY = 8, 4, 2
NXY = NX * NY
NCORE = 2
SCALE = 1.0 / math.sqrt(HEAD_DIM)
LOG2E_SCALE = math.log2(math.e) * SCALE
MESH = pl.DeviceIdType.MESH
F32 = jnp.float32
BF16 = jnp.bfloat16
NT = (((1,), (1,)), ((), ()))
NN = (((1,), (0,)), ((), ()))


def dot(a, b, dims):
    return lax.dot_general(a, b, dims, preferred_element_type=F32)


Z_AT = [0, 1, -1, 2, -2, 3, -3, 4]
XY_AT = [(0, 0), (0, 1), (1, 0), (-1, 0), (1, 1), (-1, 1), (2, 0), (2, 1)]


def kernel(
    q_in,
    k_in,
    v_in,
    do_in,
    oq,
    ok,
    ov,
    qd,
    kv,
    scores,
    dprobs,
    probs_low,
    d_low,
    kt,
    qdf,
    st_own,
    st_all,
    lse,
    delta,
    factor,
    pkv,
    dq_own,
    xsend,
    xrecv,
    zsend,
    zrecv,
    ysum,
    yrecv,
    fin,
    fin_q,
    local_sem,
    send_sem,
    recv_sem,
):
    rows = q_in.shape[0]
    total_q = NZ * rows
    total_k = NXY * rows
    seq = lax.axis_index("seq")
    head = lax.axis_index("head")
    z = seq // NXY
    x = (seq // NY) % NX
    y = seq % NY

    def at(dz=0, dx=0, dy=0):
        zz = (z + dz + NZ) % NZ
        xx = (x + dx + NX) % NX
        yy = (y + dy) % NY
        return (zz * NXY + xx * NY + yy, head)

    def head_at(dh):
        return (seq, (head + dh) % (2 * NCORE))

    counter = [0]
    sent = []

    def remote(src, dst, device):
        i = counter[0]
        counter[0] += 1
        c = pltpu.make_async_remote_copy(
            src_ref=src,
            dst_ref=dst,
            send_sem=send_sem.at[i],
            recv_sem=recv_sem.at[i],
            device_id=device,
            device_id_type=MESH,
        )
        sent.append(c)
        return c

    own = [
        pltpu.make_async_copy(src, dst, local_sem.at[i])
        for i, (src, dst) in enumerate(
            [
                (q_in, qd.at[0, 0]),
                (do_in, qd.at[1, 0]),
                (k_in, kv.at[0, 0]),
                (v_in, kv.at[1, 0]),
            ]
        )
    ]
    for c in own:
        c.start()

    barrier = pltpu.get_barrier_semaphore()
    peers = [at(dz=1), at(dz=-1), at(dx=1), at(dx=-1), at(dx=2), at(dy=1)]
    peers += [head_at(d) for d in range(1, 2 * NCORE)]
    for p in peers:
        pl.semaphore_signal(barrier, inc=1, device_id=p, device_id_type=MESH)
    for c in own:
        c.wait()
    pl.semaphore_wait(barrier, len(peers))

    qb = 2 * rows
    nq = NZ // 2
    half = rows // 2
    zc, kc = {}, {}

    def z_send(a, b, part, h):
        rs = pl.ds(h * half, half)
        c = remote(qd.at[part, a, rs], qd.at[part, b, rs], at(dz=-1 if b in (1, 3, 5) or (b == 7 and part) else 1))
        zc[b, part, h] = c
        c.start()

    def z_round(a, h_part, h):
        zc[a, h_part, h].wait_recv()
        if a < 6:
            z_send(a, a + 2, h_part, h)
        elif h_part == 0:
            z_send(a, 7, h_part, h)
        zc[a - 1, h_part, h].wait_recv()
        if a < 6:
            z_send(a - 1, a + 1, h_part, h)
        elif h_part == 1:
            z_send(a - 1, 7, h_part, h)

    def k_send(a, b, part, device):
        c = remote(kv.at[part, a], kv.at[part, b], device)
        kc[b, part] = c
        c.start()

    for part in range(2):
        for h in range(2):
            z_send(0, 2, part, h)
            z_send(0, 1, part, h)
        k_send(0, 1, part, at(dy=1))
        k_send(0, 3, part, at(dx=1))
        k_send(0, 2, part, at(dx=-1))
    for part in range(2):
        k_send(0, 6, part, at(dx=2))

    st_base = counter[0]
    counter[0] += nq * (NZ - 1)

    def stat_copy(i, d):
        k = st_base + i * (NZ - 1) + d - 1
        return pltpu.make_async_remote_copy(
            src_ref=st_own.at[i],
            dst_ref=st_all.at[d, i],
            send_sem=send_sem.at[k],
            recv_sem=recv_sem.at[k],
            device_id=at(dz=d),
            device_id_type=MESH,
        )

    def block(i, k0, kn):
        first, last = k0 == 0, k0 + kn == NXY
        qs = pl.ds(pl.multiple_of(i * qb, qb), qb)
        ks = pl.ds(k0 * rows, kn * rows)
        two = pl.ds(pl.multiple_of(i * 2, 2), 2)
        qq = qd[0, two].reshape(qb, HEAD_DIM)
        dd = qd[1, two].reshape(qb, HEAD_DIM)
        s = dot(kv[0, pl.ds(k0, kn)].reshape(kn * rows, HEAD_DIM), qq, NT)
        scores[ks, qs] = s
        m = jnp.max(s, axis=0, keepdims=True) * LOG2E_SCALE
        if not first:
            old = lse[:, qs]
            m = jnp.maximum(m, old)
        e = jnp.exp2(s * LOG2E_SCALE - m)
        dp = dot(kv[1, pl.ds(k0, kn)].reshape(kn * rows, HEAD_DIM), dd, NT)
        dprobs[ks, qs] = dp
        l = jnp.sum(e, axis=0, keepdims=True)
        w = jnp.sum(e * dp, axis=0, keepdims=True)
        if not first:
            fade = jnp.exp2(old - m)
            l += fade * factor[:, qs]
            w += fade * delta[:, qs]
        if last:
            m = m + jnp.log2(l)
            w = w / l
            for r in range(4):
                st_own[i, pl.ds(r, 1), :] = m[:, r * 128 : (r + 1) * 128]
                st_own[i, pl.ds(4 + r, 1), :] = w[:, r * 128 : (r + 1) * 128]
            for d in range(1, NZ):
                stat_copy(i, d).start()
        else:
            factor[:, qs] = l
            delta[:, qs] = w
        lse[:, qs] = m

    def spread(part):
        kc[1, part].wait_recv()
        k_send(1, 5, part, at(dx=1))
        k_send(1, 4, part, at(dx=-1))

    z_round(2, 0, 0)
    z_round(2, 0, 1)
    spread(0)
    z_round(2, 1, 0)
    z_round(2, 1, 1)
    spread(1)
    for part in range(2):
        kc[2, part].wait_recv()
        kc[3, part].wait_recv()
    block(0, 0, NXY // 2)
    for part in range(2):
        kc[6, part].wait_recv()
        k_send(6, 7, part, at(dy=1))
        z_round(4, part, 0)
        z_round(4, part, 1)
    block(1, 0, NXY // 2)
    for part in range(2):
        z_round(6, part, 0)
        z_round(6, part, 1)
    block(2, 0, NXY // 2)
    for part in range(2):
        for slot in (4, 5, 7):
            kc[slot, part].wait_recv()

    @pl.loop(0, nq - 1)
    def _(i):
        block(i, NXY // 2, NXY // 2)

    for part in range(2):
        for h in range(2):
            zc[7, part, h].wait_recv()
    block(nq - 1, 0, NXY)

    for j in range(NXY):
        kt[:, pl.ds(j * rows, rows)] = kv[0, j].T

    @pl.loop(0, NXY)
    def _(j):
        ks = pl.ds(pl.multiple_of(j * rows, rows), rows)
        p = jnp.exp2(scores[ks, :] * LOG2E_SCALE - lse[...])
        scores[ks, :] = p
        probs_low[ks, :] = p.astype(BF16)

    st_all[0] = st_own[...]
    for i in range(nq):
        for d in range(1, NZ):
            stat_copy(i, d).wait_recv()
    for slot, dz in enumerate(Z_AT):
        tops, deltas = [], []
        for d in range(NZ):
            there = Z_AT.index((dz + d + 3) % NZ - 3)
            i, b = there // 2, there % 2
            tops.append(st_all[d, i, pl.ds(2 * b, 2), :])
            deltas.append(st_all[d, i, pl.ds(4 + 2 * b, 2), :])
        big = tops[0]
        for t in tops[1:]:
            big = jnp.maximum(big, t)
        mass = jnp.zeros_like(big)
        weighted = jnp.zeros_like(big)
        for t, w in zip(tops, deltas):
            f = jnp.exp2(t - big)
            mass += f
            weighted += f * w
        weighted = weighted / mass
        own_factor = jnp.exp2(tops[0] - (big + jnp.log2(mass)))
        for r in range(2):
            cols = pl.ds(slot * rows + r * 128, 128)
            delta[:, cols] = weighted[r : r + 1, :]
            factor[:, cols] = own_factor[r : r + 1, :]
        wide = jnp.broadcast_to(
            factor[:, pl.ds(slot * rows, rows)], (HEAD_DIM, rows)
        ).T
        for part in range(2):
            qdf[part, slot] = (qd[part, slot].astype(F32) * wide).astype(BF16)

    xc = {}
    for part in (1, 0):
        for slot in range(2, NXY):
            dx, dy = XY_AT[slot]
            xc[part, slot] = remote(
                xsend.at[part, slot], xrecv.at[part, slot], at(dx=dx)
            )
    zc2 = {
        slot: remote(zsend.at[slot], zrecv.at[slot], at(dz=Z_AT[slot]))
        for slot in range(1, NZ)
    }

    def key_side(part, left, high, low):
        @pl.loop(0, high - low)
        def _(it):
            slot = high - 1 - it
            ks = pl.ds(pl.multiple_of(slot * rows, rows), rows)
            t = dot(left[ks, :], qdf[part].reshape(total_q, HEAD_DIM), NN)
            if part == 0:
                t = t * SCALE
            xsend[part, slot] = t.astype(BF16)
            if low == 0:

                @pl.when(slot < 2)
                def _():
                    pkv[part, jnp.minimum(slot, 1)] = t

            for s in range(max(low, 2), high):

                @pl.when(slot == s)
                def _():
                    xc[part, s].start()

    def query_side(high, low):
        @pl.loop(0, high - low)
        def _(it):
            i = high - 1 - it
            qs = pl.ds(pl.multiple_of(i * qb, qb), qb)
            ds = (scores[:, qs] * (dprobs[:, qs] - delta[:, qs])).astype(BF16)
            d_low[:, qs] = ds
            t = dot(kt[...], ds, NN) * (factor[:, qs] * SCALE)
            for b in range(2):
                mine = t[:, b * rows : (b + 1) * rows].T
                zsend[i * 2 + b] = mine.astype(BF16)
                if low == 0 and b == 0:

                    @pl.when(i == 0)
                    def _():
                        dq_own[...] = mine

            for s in range(max(2 * low, 1), 2 * high):

                @pl.when(i == s // 2)
                def _():
                    zc2[s].start()

    key_side(1, probs_low, 8, 6)
    query_side(4, 2)
    key_side(1, probs_low, 6, 0)
    query_side(2, 0)
    key_side(0, d_low, 8, 0)

    def up(ref):
        return ref.astype(F32)

    yc = {}

    def over_x(part):
        for dy in (1, 0):
            total = pkv[part, dy]
            for slot in range(2, NXY):
                if XY_AT[slot][1] == dy:
                    xc[part, slot].wait_recv()
                    total += up(xrecv[part, slot])
            ysum[part, dy] = total.astype(BF16)
            seq_to, _ = at(dy=dy)
            far = (head + NCORE) % (2 * NCORE)
            if dy:
                yc[part, 0] = remote(
                    ysum.at[part, 1], yrecv.at[part, 0], (seq_to, head)
                )
                yc[part, 0].start()
            yc[part, 1 + dy] = remote(
                ysum.at[part, dy], yrecv.at[part, 1 + dy], (seq_to, far)
            )
            yc[part, 1 + dy].start()

    def columns(out, h):
        return out.at[
            :, pl.ds(pl.multiple_of(h * HEAD_DIM, HEAD_DIM), HEAD_DIM)
        ]

    ends = []
    other = head + 1 - 2 * (head % 2)

    def over_y(part, out):
        yc[part, 0].wait_recv()
        fin[part, 0] = (up(ysum[part, 0]) + up(yrecv[part, 0])).astype(BF16)
        yc[part, 1].wait_recv()
        yc[part, 2].wait_recv()
        fin[part, 1] = (up(yrecv[part, 1]) + up(yrecv[part, 2])).astype(BF16)
        for b in range(2):
            cols = columns(out, (head + NCORE * b) % (2 * NCORE))
            c = remote(fin.at[part, b], cols, (seq, other))
            c.start()
            ends.append(c.wait_recv)
            c = pltpu.make_async_copy(fin.at[part, b], cols, local_sem.at[2 * part + b])
            c.start()
            ends.append(c.wait)

    over_x(1)
    over_x(0)
    over_y(1, ov)
    total = dq_own[...]
    for slot in range(1, NZ):
        zc2[slot].wait_recv()
        total += up(zrecv[slot])
    fin_q[...] = total.astype(BF16)
    cols = columns(oq, head)
    for d in range(1, 2 * NCORE):
        c = remote(fin_q, cols, head_at(d))
        c.start()
        ends.append(c.wait_recv)
    c = pltpu.make_async_copy(fin_q, cols, local_sem.at[4])
    c.start()
    ends.append(c.wait)
    over_y(0, ok)
    for wait in ends:
        wait()
    for c in sent:
        c.wait_send()
    for i in range(nq):
        for d in range(1, NZ):
            stat_copy(i, d).wait_send()


def hand_over(a, b, c, oa, ob, oc):
    oa[...] = a[...]
    ob[...] = b[...]
    oc[...] = c[...]


def local(queries, keys, values, d_out):
    rows, width = queries.shape
    total = NZ * rows
    any_spec = pl.BlockSpec(memory_space=pl.ANY)
    out = jax.ShapeDtypeStruct((rows, 2 * NCORE * width), BF16)
    vm = pltpu.VMEM
    outs = pl.pallas_call(
        kernel,
        out_shape=[out, out, out],
        in_specs=[any_spec] * 4,
        out_specs=[any_spec] * 3,
        scratch_shapes=[
            vm((2, NZ, rows, width), BF16),
            vm((2, NXY, rows, width), BF16),
            vm((total, total), F32),
            vm((total, total), F32),
            vm((total, total), BF16),
            vm((total, total), BF16),
            vm((width, total), BF16),
            vm((2, NZ, rows, width), BF16),
            vm((NZ // 2, 8, 128), F32),
            vm((NZ, NZ // 2, 8, 128), F32),
            vm((1, total), F32),
            vm((1, total), F32),
            vm((1, total), F32),
            vm((2, 2, rows, width), F32),
            vm((rows, width), F32),
            vm((2, NXY, rows, width), BF16),
            vm((2, NXY, rows, width), BF16),
            vm((NZ, rows, width), BF16),
            vm((NZ, rows, width), BF16),
            vm((2, 2, rows, width), BF16),
            vm((2, 3, rows, width), BF16),
            vm((2, 2, rows, width), BF16),
            vm((rows, width), BF16),
            pltpu.SemaphoreType.DMA((5,)),
            pltpu.SemaphoreType.DMA((112,)),
            pltpu.SemaphoreType.DMA((112,)),
        ],
        compiler_params=pltpu.CompilerParams(
            collective_id=0, has_side_effects=True, vmem_limit_bytes=63 * 2**20
        ),
        name="attention_backward",
    )(queries, keys, values, d_out)
    spec = pl.BlockSpec(memory_space=pltpu.VMEM)
    return pl.pallas_call(
        hand_over,
        out_shape=[out, out, out],
        in_specs=[spec] * 3,
        out_specs=[spec] * 3,
        name="hand_over",
    )(*outs)


def solution(mesh):
    in_specs = (P("seq", "head"), P("seq", "head"), P("seq", "head"), P("seq", "head"))
    out_specs = (P("seq", None), P("seq", None), P("seq", None))
    return jax.shard_map(local, mesh=mesh, in_specs=in_specs, out_specs=out_specs, check_vma=False)
```

```python
import math

import jax
import jax.numpy as jnp
from jax import lax
from jax.experimental import pallas as pl
from jax.experimental.pallas import tpu as pltpu
from jax.sharding import PartitionSpec as P

HEAD_DIM = 128
NZ, NX, NY = 8, 4, 2
NXY = NX * NY
NCORE = 2
SCALE = 1.0 / math.sqrt(HEAD_DIM)
LOG2E_SCALE = math.log2(math.e) * SCALE
MESH = pl.DeviceIdType.MESH
F32 = jnp.float32
BF16 = jnp.bfloat16
NT = (((1,), (1,)), ((), ()))
NN = (((1,), (0,)), ((), ()))


def dot(a, b, dims):
    return lax.dot_general(a, b, dims, preferred_element_type=F32)


Z_AT = [0, 1, -1, 2, -2, 3, -3, 4]
XY_AT = [(0, 0), (0, 1), (1, 0), (-1, 0), (2, 0), (1, 1), (-1, 1), (2, 1)]


def kernel(
    q_in,
    k_in,
    v_in,
    do_in,
    oq,
    ok,
    ov,
    qd,
    kv,
    scores,
    dprobs,
    probs_low,
    d_low,
    kt,
    qdf,
    st_own,
    st_all,
    lse,
    delta,
    factor,
    pkv,
    dq_own,
    xsend,
    xrecv,
    zsend,
    zrecv,
    ysum,
    yrecv,
    fin,
    fin_q,
    local_sem,
    send_sem,
    recv_sem,
):
    rows = q_in.shape[0]
    total_q = NZ * rows
    total_k = NXY * rows
    seq = lax.axis_index("seq")
    head = lax.axis_index("head")
    z = seq // NXY
    x = (seq // NY) % NX
    y = seq % NY

    def at(dz=0, dx=0, dy=0):
        zz = (z + dz + NZ) % NZ
        xx = (x + dx + NX) % NX
        yy = (y + dy) % NY
        return (zz * NXY + xx * NY + yy, head)

    def head_at(dh):
        return (seq, (head + dh) % (2 * NCORE))

    counter = [0]
    sent = []

    def remote(src, dst, device):
        i = counter[0]
        counter[0] += 1
        c = pltpu.make_async_remote_copy(
            src_ref=src,
            dst_ref=dst,
            send_sem=send_sem.at[i],
            recv_sem=recv_sem.at[i],
            device_id=device,
            device_id_type=MESH,
        )
        sent.append(c)
        return c

    own = [
        pltpu.make_async_copy(src, dst, local_sem.at[i])
        for i, (src, dst) in enumerate(
            [
                (q_in, qd.at[0, 0]),
                (do_in, qd.at[1, 0]),
                (k_in, kv.at[0, 0]),
                (v_in, kv.at[1, 0]),
            ]
        )
    ]
    for c in own:
        c.start()

    barrier = pltpu.get_barrier_semaphore()
    peers = [at(dz=1), at(dz=-1), at(dx=1), at(dx=-1), at(dx=2), at(dy=1)]
    peers += [head_at(d) for d in range(1, 2 * NCORE)]
    for p in peers:
        pl.semaphore_signal(barrier, inc=1, device_id=p, device_id_type=MESH)
    for c in own:
        c.wait()
    pl.semaphore_wait(barrier, len(peers))

    qb = 2 * rows
    nq = NZ // 2
    half = rows // 2
    zc, kc = {}, {}

    def z_send(a, b, part, h, dz):
        rs = pl.ds(h * half, half)
        c = remote(qd.at[part, a, rs], qd.at[part, b, rs], at(dz=dz))
        zc[b, part, h] = c
        c.start()

    def z_round(a, part, h):
        zc[a, part, h].wait_recv()
        z_send(a, a + 2, part, h, 1)
        zc[a - 1, part, h].wait_recv()
        z_send(a - 1, a + 1, part, h, -1)
        if a == 4:
            if part == 0:
                z_send(4, 7, part, h, 2)
            else:
                z_send(3, 7, part, h, -2)

    def k_send(a, b, part, device):
        c = remote(kv.at[part, a], kv.at[part, b], device)
        kc[b, part] = c
        c.start()

    for part in range(2):
        for h in range(2):
            z_send(0, 2, part, h, 1)
            z_send(0, 1, part, h, -1)
        k_send(0, 1, part, at(dy=1))
        k_send(0, 3, part, at(dx=1))
        k_send(0, 2, part, at(dx=-1))
    for part in range(2):
        k_send(0, 4, part, at(dx=2))

    groups = ((0, 5), (5, 2), (7, 1))
    st_base = counter[0]
    counter[0] += len(groups) * (NZ - 1)

    def stat_copy(g, d):
        k = st_base + g * (NZ - 1) + d - 1
        slots = pl.ds(*groups[g])
        return pltpu.make_async_remote_copy(
            src_ref=st_own.at[slots],
            dst_ref=st_all.at[d, slots],
            send_sem=send_sem.at[k],
            recv_sem=recv_sem.at[k],
            device_id=at(dz=d),
            device_id_type=MESH,
        )

    def block(c0, cn, k0, kn):
        first, last = k0 == 0, k0 + kn == NXY
        qs = pl.ds(c0 * rows, cn * rows)
        ks = pl.ds(k0 * rows, kn * rows)
        slots = pl.ds(c0, cn)
        qq = qd[0, slots].reshape(cn * rows, HEAD_DIM)
        dd = qd[1, slots].reshape(cn * rows, HEAD_DIM)
        s = dot(kv[0, pl.ds(k0, kn)].reshape(kn * rows, HEAD_DIM), qq, NT)
        scores[ks, qs] = s
        m = jnp.max(s, axis=0, keepdims=True) * LOG2E_SCALE
        if not first:
            old = lse[:, qs]
            m = jnp.maximum(m, old)
        e = jnp.exp2(s * LOG2E_SCALE - m)
        dp = dot(kv[1, pl.ds(k0, kn)].reshape(kn * rows, HEAD_DIM), dd, NT)
        dprobs[ks, qs] = dp
        l = jnp.sum(e, axis=0, keepdims=True)
        w = jnp.sum(e * dp, axis=0, keepdims=True)
        if not first:
            fade = jnp.exp2(old - m)
            l += fade * factor[:, qs]
            w += fade * delta[:, qs]
        if last:
            m = m + jnp.log2(l)
            w = w / l
            for c in range(cn):
                for r in range(2):
                    lanes = slice((2 * c + r) * 128, (2 * c + r + 1) * 128)
                    st_own[c0 + c, pl.ds(r, 1), :] = m[:, lanes]
                    st_own[c0 + c, pl.ds(2 + r, 1), :] = w[:, lanes]
        else:
            factor[:, qs] = l
            delta[:, qs] = w
        lse[:, qs] = m

    def spread(part):
        kc[1, part].wait_recv()
        k_send(1, 6, part, at(dx=1))
        k_send(1, 5, part, at(dx=-1))

    def far_keys(part):
        kc[4, part].wait_recv()
        k_send(4, 7, part, at(dy=1))

    z_round(2, 0, 0)
    z_round(2, 0, 1)
    z_round(2, 1, 0)
    spread(0)
    z_round(2, 1, 1)
    spread(1)
    for part in range(2):
        kc[2, part].wait_recv()
        kc[3, part].wait_recv()
    block(0, 3, 0, 4)
    z_round(4, 0, 0)
    z_round(4, 0, 1)
    far_keys(0)
    z_round(4, 1, 0)
    z_round(4, 1, 1)
    far_keys(1)
    block(3, 2, 0, 4)
    for part in range(2):
        kc[5, part].wait_recv()
        kc[6, part].wait_recv()
    block(0, 3, 4, 3)
    block(3, 2, 4, 3)
    kc[7, 0].wait_recv()
    kc[7, 1].wait_recv()
    block(0, 5, 7, 1)
    for part in range(2):
        for h in range(2):
            zc[6, part, h].wait_recv()
            zc[5, part, h].wait_recv()
    for d in (1, 7, 2, 6, 3, 5):
        stat_copy(0, d).start()
    block(5, 2, 0, NXY)
    for part in range(2):
        for h in range(2):
            zc[7, part, h].wait_recv()
    stat_copy(0, 4).start()
    for d in (4, 3, 5, 2, 6, 1, 7):
        stat_copy(1, d).start()
    block(7, 1, 0, NXY)
    for d in (4, 3, 5, 2, 6, 1, 7):
        stat_copy(2, d).start()

    for j in range(NXY):
        kt[:, pl.ds(j * rows, rows)] = kv[0, j].T

    @pl.loop(0, NXY)
    def _(j):
        ks = pl.ds(pl.multiple_of(j * rows, rows), rows)
        p = jnp.exp2(scores[ks, :] * LOG2E_SCALE - lse[...])
        scores[ks, :] = p
        probs_low[ks, :] = p.astype(BF16)

    st_all[0] = st_own[...]
    for g in range(len(groups)):
        for d in range(1, NZ):
            stat_copy(g, d).wait_recv()
    for slot, dz in enumerate(Z_AT):
        tops, deltas = [], []
        for d in range(NZ):
            there = Z_AT.index((dz + d + 3) % NZ - 3)
            tops.append(st_all[d, there, pl.ds(0, 2), :])
            deltas.append(st_all[d, there, pl.ds(2, 2), :])
        big = tops[0]
        for t in tops[1:]:
            big = jnp.maximum(big, t)
        mass = jnp.zeros_like(big)
        weighted = jnp.zeros_like(big)
        for t, w in zip(tops, deltas):
            f = jnp.exp2(t - big)
            mass += f
            weighted += f * w
        weighted = weighted / mass
        own_factor = jnp.exp2(tops[0] - (big + jnp.log2(mass)))
        for r in range(2):
            cols = pl.ds(slot * rows + r * 128, 128)
            delta[:, cols] = weighted[r : r + 1, :]
            factor[:, cols] = own_factor[r : r + 1, :]
        wide = jnp.broadcast_to(
            factor[:, pl.ds(slot * rows, rows)], (HEAD_DIM, rows)
        ).T
        for part in range(2):
            qdf[part, slot] = (qd[part, slot].astype(F32) * wide).astype(BF16)

    xc = {}
    for part in (1, 0):
        for slot in range(2, NXY):
            dx, dy = XY_AT[slot]
            xc[part, slot] = remote(
                xsend.at[part, slot], xrecv.at[part, slot], at(dx=dx)
            )
    zc2 = {
        slot: remote(zsend.at[slot], zrecv.at[slot], at(dz=Z_AT[slot]))
        for slot in range(1, NZ)
    }

    def key_side(part, left, high, low):
        @pl.loop(0, (high - low) // 2)
        def _(it):
            slot = high - 2 - 2 * it
            ks = pl.ds(pl.multiple_of(slot * rows, rows), 2 * rows)
            t = dot(left[ks, :], qdf[part].reshape(total_q, HEAD_DIM), NN)
            if part == 0:
                t = t * SCALE
            t = t.reshape(2, rows, HEAD_DIM)
            if low == 0:

                @pl.when(slot == 0)
                def _():
                    pkv[part] = t

            xsend[part, pl.ds(slot, 2)] = t.astype(BF16)
            for s in range(max(low, 2), high, 2):

                @pl.when(slot == s)
                def _():
                    xc[part, s + 1].start()
                    xc[part, s].start()

    def query_side(high, low):
        @pl.loop(0, high - low)
        def _(it):
            i = high - 1 - it
            qs = pl.ds(pl.multiple_of(i * qb, qb), qb)
            ds = (scores[:, qs] * (dprobs[:, qs] - delta[:, qs])).astype(BF16)
            d_low[:, qs] = ds
            t = dot(kt[...], ds, NN) * (factor[:, qs] * SCALE)
            for b in range(2):
                mine = t[:, b * rows : (b + 1) * rows].T
                zsend[i * 2 + b] = mine.astype(BF16)
                if low == 0 and b == 0:

                    @pl.when(i == 0)
                    def _():
                        dq_own[...] = mine

            for s in range(max(2 * low, 1), 2 * high):

                @pl.when(i == s // 2)
                def _():
                    zc2[s].start()

    key_side(1, probs_low, 8, 2)
    query_side(4, 0)
    key_side(0, d_low, 8, 2)
    key_side(1, probs_low, 2, 0)
    key_side(0, d_low, 2, 0)

    def up(ref):
        return ref.astype(F32)

    yc = {}

    def over_x(part):
        for dy in (1, 0):
            total = pkv[part, dy]
            for slot in range(2, NXY):
                if XY_AT[slot][1] == dy:
                    xc[part, slot].wait_recv()
                    total += up(xrecv[part, slot])
            ysum[part, dy] = total.astype(BF16)
            seq_to, _ = at(dy=dy)
            far = (head + NCORE) % (2 * NCORE)
            if dy:
                yc[part, 0] = remote(
                    ysum.at[part, 1], yrecv.at[part, 0], (seq_to, head)
                )
                yc[part, 0].start()
            yc[part, 1 + dy] = remote(
                ysum.at[part, dy], yrecv.at[part, 1 + dy], (seq_to, far)
            )
            yc[part, 1 + dy].start()

    def columns(out, h):
        return out.at[
            :, pl.ds(pl.multiple_of(h * HEAD_DIM, HEAD_DIM), HEAD_DIM)
        ]

    ends = []
    other = head + 1 - 2 * (head % 2)

    def over_y(part, out):
        yc[part, 0].wait_recv()
        fin[part, 0] = (up(ysum[part, 0]) + up(yrecv[part, 0])).astype(BF16)
        yc[part, 1].wait_recv()
        yc[part, 2].wait_recv()
        fin[part, 1] = (up(yrecv[part, 1]) + up(yrecv[part, 2])).astype(BF16)
        for b in range(2):
            cols = columns(out, (head + NCORE * b) % (2 * NCORE))
            c = remote(fin.at[part, b], cols, (seq, other))
            c.start()
            ends.append(c.wait_recv)
            c = pltpu.make_async_copy(fin.at[part, b], cols, local_sem.at[2 * part + b])
            c.start()
            ends.append(c.wait)

    over_x(1)
    over_x(0)
    over_y(1, ov)
    total = dq_own[...]
    for slot in range(1, NZ):
        zc2[slot].wait_recv()
        total += up(zrecv[slot])
    fin_q[...] = total.astype(BF16)
    cols = columns(oq, head)
    for d in range(1, 2 * NCORE):
        c = remote(fin_q, cols, head_at(d))
        c.start()
        ends.append(c.wait_recv)
    c = pltpu.make_async_copy(fin_q, cols, local_sem.at[4])
    c.start()
    ends.append(c.wait)
    over_y(0, ok)
    for wait in ends:
        wait()
    for c in sent:
        c.wait_send()
    for g in range(len(groups)):
        for d in range(1, NZ):
            stat_copy(g, d).wait_send()


def hand_over(a, b, c, oa, ob, oc):
    oa[...] = a[...]
    ob[...] = b[...]
    oc[...] = c[...]


def local(queries, keys, values, d_out):
    rows, width = queries.shape
    total = NZ * rows
    any_spec = pl.BlockSpec(memory_space=pl.ANY)
    out = jax.ShapeDtypeStruct((rows, 2 * NCORE * width), BF16)
    vm = pltpu.VMEM
    outs = pl.pallas_call(
        kernel,
        out_shape=[out, out, out],
        in_specs=[any_spec] * 4,
        out_specs=[any_spec] * 3,
        scratch_shapes=[
            vm((2, NZ, rows, width), BF16),
            vm((2, NXY, rows, width), BF16),
            vm((total, total), F32),
            vm((total, total), F32),
            vm((total, total), BF16),
            vm((total, total), BF16),
            vm((width, total), BF16),
            vm((2, NZ, rows, width), BF16),
            vm((NZ, 4, 128), F32),
            vm((NZ, NZ, 4, 128), F32),
            vm((1, total), F32),
            vm((1, total), F32),
            vm((1, total), F32),
            vm((2, 2, rows, width), F32),
            vm((rows, width), F32),
            vm((2, NXY, rows, width), BF16),
            vm((2, NXY, rows, width), BF16),
            vm((NZ, rows, width), BF16),
            vm((NZ, rows, width), BF16),
            vm((2, 2, rows, width), BF16),
            vm((2, 3, rows, width), BF16),
            vm((2, 2, rows, width), BF16),
            vm((rows, width), BF16),
            pltpu.SemaphoreType.DMA((5,)),
            pltpu.SemaphoreType.DMA((112,)),
            pltpu.SemaphoreType.DMA((112,)),
        ],
        compiler_params=pltpu.CompilerParams(
            collective_id=0, has_side_effects=True, vmem_limit_bytes=63 * 2**20
        ),
        name="attention_backward",
    )(queries, keys, values, d_out)
    spec = pl.BlockSpec(memory_space=pltpu.VMEM)
    return pl.pallas_call(
        hand_over,
        out_shape=[out, out, out],
        in_specs=[spec] * 3,
        out_specs=[spec] * 3,
        name="hand_over",
    )(*outs)


def solution(mesh):
    in_specs = (P("seq", "head"), P("seq", "head"), P("seq", "head"), P("seq", "head"))
    out_specs = (P("seq", None), P("seq", None), P("seq", None))
    return jax.shard_map(local, mesh=mesh, in_specs=in_specs, out_specs=out_specs, check_vma=False)
```

```python
import math

import jax
import jax.numpy as jnp
from jax import lax
from jax.experimental import pallas as pl
from jax.experimental.pallas import tpu as pltpu
from jax.sharding import PartitionSpec as P

HEAD_DIM = 128
NZ, NX, NY = 8, 4, 2
NXY = NX * NY
NCORE = 2
SCALE = 1.0 / math.sqrt(HEAD_DIM)
LOG2E_SCALE = math.log2(math.e) * SCALE
MESH = pl.DeviceIdType.MESH
F32 = jnp.float32
BF16 = jnp.bfloat16
NT = (((1,), (1,)), ((), ()))
NN = (((1,), (0,)), ((), ()))


def dot(a, b, dims):
    return lax.dot_general(a, b, dims, preferred_element_type=F32)


Z_AT = [0, 1, -1, 2, -2, 3, -3, 4]
XY_AT = [(0, 0), (0, 1), (1, 0), (-1, 0), (2, 0), (1, 1), (-1, 1), (2, 1)]


def kernel(
    q_in,
    k_in,
    v_in,
    do_in,
    oq,
    ok,
    ov,
    qd,
    kv,
    scores,
    dprobs,
    probs_low,
    d_low,
    kt,
    qdf,
    st_own,
    st_all,
    lse,
    delta,
    factor,
    pkv,
    dq_own,
    xsend,
    xrecv,
    zsend,
    zrecv,
    ysum,
    yrecv,
    fin,
    fin_q,
    local_sem,
    send_sem,
    recv_sem,
):
    rows = q_in.shape[0]
    total_q = NZ * rows
    total_k = NXY * rows
    seq = lax.axis_index("seq")
    head = lax.axis_index("head")
    z = seq // NXY
    x = (seq // NY) % NX
    y = seq % NY

    def at(dz=0, dx=0, dy=0):
        zz = (z + dz + NZ) % NZ
        xx = (x + dx + NX) % NX
        yy = (y + dy) % NY
        return (zz * NXY + xx * NY + yy, head)

    def head_at(dh):
        return (seq, (head + dh) % (2 * NCORE))

    counter = [0]
    sent = []

    def remote(src, dst, device):
        i = counter[0]
        counter[0] += 1
        c = pltpu.make_async_remote_copy(
            src_ref=src,
            dst_ref=dst,
            send_sem=send_sem.at[i],
            recv_sem=recv_sem.at[i],
            device_id=device,
            device_id_type=MESH,
        )
        sent.append(c)
        return c

    def all_sent():
        while sent:
            sent.pop().wait_send()

    own = [
        pltpu.make_async_copy(src, dst, local_sem.at[i])
        for i, (src, dst) in enumerate(
            [
                (q_in, qd.at[0, 0]),
                (do_in, qd.at[1, 0]),
                (k_in, kv.at[0, 0]),
                (v_in, kv.at[1, 0]),
            ]
        )
    ]
    for c in own:
        c.start()

    barrier = pltpu.get_barrier_semaphore()
    peers = [at(dz=1), at(dz=-1), at(dx=1), at(dx=-1), at(dx=2), at(dy=1)]
    peers += [head_at(d) for d in range(1, 2 * NCORE)]
    for p in peers:
        pl.semaphore_signal(barrier, inc=1, device_id=p, device_id_type=MESH)
    for c in own:
        c.wait()
    pl.semaphore_wait(barrier, len(peers))

    qb = 2 * rows
    nq = NZ // 2
    half = rows // 2
    zc, kc = {}, {}

    def z_send(a, b, part, h, dz):
        rs = pl.ds(h * half, half)
        c = remote(qd.at[part, a, rs], qd.at[part, b, rs], at(dz=dz))
        zc[b, part, h] = c
        c.start()

    def z_round(a, part, h):
        zc[a, part, h].wait_recv()
        z_send(a, a + 2, part, h, 1)
        zc[a - 1, part, h].wait_recv()
        z_send(a - 1, a + 1, part, h, -1)
        if a == 4:
            if part == 0:
                z_send(4, 7, part, h, 2)
            else:
                z_send(3, 7, part, h, -2)

    def k_send(a, b, part, device):
        c = remote(kv.at[part, a], kv.at[part, b], device)
        kc[b, part] = c
        c.start()

    for part in range(2):
        for h in range(2):
            z_send(0, 2, part, h, 1)
            z_send(0, 1, part, h, -1)
        k_send(0, 1, part, at(dy=1))
        k_send(0, 3, part, at(dx=1))
        k_send(0, 2, part, at(dx=-1))
    for part in range(2):
        k_send(0, 4, part, at(dx=2))

    groups = ((0, 5), (5, 2), (7, 1))
    st_base = counter[0]
    counter[0] += len(groups) * (NZ - 1)

    def stat_copy(g, d):
        k = st_base + g * (NZ - 1) + d - 1
        slots = pl.ds(*groups[g])
        return pltpu.make_async_remote_copy(
            src_ref=st_own.at[slots],
            dst_ref=st_all.at[d, slots],
            send_sem=send_sem.at[k],
            recv_sem=recv_sem.at[k],
            device_id=at(dz=d),
            device_id_type=MESH,
        )

    def block(c0, cn, k0, kn):
        first, last = k0 == 0, k0 + kn == NXY
        qs = pl.ds(c0 * rows, cn * rows)
        ks = pl.ds(k0 * rows, kn * rows)
        slots = pl.ds(c0, cn)
        qq = qd[0, slots].reshape(cn * rows, HEAD_DIM)
        dd = qd[1, slots].reshape(cn * rows, HEAD_DIM)
        s = dot(kv[0, pl.ds(k0, kn)].reshape(kn * rows, HEAD_DIM), qq, NT)
        scores[ks, qs] = s
        m = jnp.max(s, axis=0, keepdims=True) * LOG2E_SCALE
        if not first:
            old = lse[:, qs]
            m = jnp.maximum(m, old)
        e = jnp.exp2(s * LOG2E_SCALE - m)
        dp = dot(kv[1, pl.ds(k0, kn)].reshape(kn * rows, HEAD_DIM), dd, NT)
        dprobs[ks, qs] = dp
        l = jnp.sum(e, axis=0, keepdims=True)
        w = jnp.sum(e * dp, axis=0, keepdims=True)
        if not first:
            fade = jnp.exp2(old - m)
            l += fade * factor[:, qs]
            w += fade * delta[:, qs]
        if last:
            m = m + jnp.log2(l)
            w = w / l
            for c in range(cn):
                for r in range(2):
                    lanes = slice((2 * c + r) * 128, (2 * c + r + 1) * 128)
                    st_own[c0 + c, pl.ds(r, 1), :] = m[:, lanes]
                    st_own[c0 + c, pl.ds(2 + r, 1), :] = w[:, lanes]
        else:
            factor[:, qs] = l
            delta[:, qs] = w
        lse[:, qs] = m

    def spread(part):
        kc[1, part].wait_recv()
        k_send(1, 6, part, at(dx=1))
        k_send(1, 5, part, at(dx=-1))

    def far_keys(part):
        kc[4, part].wait_recv()
        k_send(4, 7, part, at(dy=1))

    z_round(2, 0, 0)
    z_round(2, 0, 1)
    z_round(2, 1, 0)
    spread(0)
    z_round(2, 1, 1)
    spread(1)
    for part in range(2):
        kc[2, part].wait_recv()
        kc[3, part].wait_recv()
    z_round(4, 0, 0)
    z_round(4, 0, 1)
    far_keys(0)
    z_round(4, 1, 0)
    z_round(4, 1, 1)
    far_keys(1)
    block(0, 3, 0, 4)
    block(3, 2, 0, 4)
    for part in range(2):
        kc[5, part].wait_recv()
        kc[6, part].wait_recv()
    block(0, 3, 4, 3)
    block(3, 2, 4, 3)
    kc[7, 0].wait_recv()
    kc[7, 1].wait_recv()
    block(0, 5, 7, 1)
    for part in range(2):
        for h in range(2):
            zc[6, part, h].wait_recv()
            zc[5, part, h].wait_recv()
    for d in (1, 7, 2, 6, 3, 5):
        stat_copy(0, d).start()
    block(5, 2, 0, NXY)
    for part in range(2):
        for h in range(2):
            zc[7, part, h].wait_recv()
    stat_copy(0, 4).start()
    for d in (4, 3, 5, 2, 6, 1, 7):
        stat_copy(1, d).start()
    block(7, 1, 0, NXY)
    for d in (4, 3, 5, 2, 6, 1, 7):
        stat_copy(2, d).start()

    for j in range(NXY):
        kt[:, pl.ds(j * rows, rows)] = kv[0, j].T

    @pl.loop(0, NXY)
    def _(j):
        ks = pl.ds(pl.multiple_of(j * rows, rows), rows)
        p = jnp.exp2(scores[ks, :] * LOG2E_SCALE - lse[...])
        scores[ks, :] = p
        probs_low[ks, :] = p.astype(BF16)

    all_sent()

    st_all[0] = st_own[...]
    for g in range(len(groups)):
        for d in range(1, NZ):
            stat_copy(g, d).wait_recv()
    for slot, dz in enumerate(Z_AT):
        tops, deltas = [], []
        for d in range(NZ):
            there = Z_AT.index((dz + d + 3) % NZ - 3)
            tops.append(st_all[d, there, pl.ds(0, 2), :])
            deltas.append(st_all[d, there, pl.ds(2, 2), :])
        big = tops[0]
        for t in tops[1:]:
            big = jnp.maximum(big, t)
        mass = jnp.zeros_like(big)
        weighted = jnp.zeros_like(big)
        for t, w in zip(tops, deltas):
            f = jnp.exp2(t - big)
            mass += f
            weighted += f * w
        weighted = weighted / mass
        own_factor = jnp.exp2(tops[0] - (big + jnp.log2(mass)))
        for r in range(2):
            cols = pl.ds(slot * rows + r * 128, 128)
            delta[:, cols] = weighted[r : r + 1, :]
            factor[:, cols] = own_factor[r : r + 1, :]
        wide = jnp.broadcast_to(
            factor[:, pl.ds(slot * rows, rows)], (HEAD_DIM, rows)
        ).T
        for part in range(2):
            qdf[part, slot] = (qd[part, slot].astype(F32) * wide).astype(BF16)

    xc = {}
    for part in (1, 0):
        for slot in range(2, NXY):
            dx, dy = XY_AT[slot]
            xc[part, slot] = remote(
                xsend.at[part, slot], xrecv.at[part, slot], at(dx=dx)
            )
    zc2 = {
        slot: remote(zsend.at[slot], zrecv.at[slot], at(dz=Z_AT[slot]))
        for slot in range(1, NZ)
    }

    def key_side(part, left, high, low):
        @pl.loop(0, (high - low) // 2)
        def _(it):
            slot = high - 2 - 2 * it
            ks = pl.ds(pl.multiple_of(slot * rows, rows), 2 * rows)
            t = dot(left[ks, :], qdf[part].reshape(total_q, HEAD_DIM), NN)
            if part == 0:
                t = t * SCALE
            t = t.reshape(2, rows, HEAD_DIM)
            if low == 0:

                @pl.when(slot == 0)
                def _():
                    pkv[part] = t

            xsend[part, pl.ds(slot, 2)] = t.astype(BF16)
            for s in range(max(low, 2), high, 2):

                @pl.when(slot == s)
                def _():
                    xc[part, s + 1].start()
                    xc[part, s].start()

    def query_side(high, low):
        @pl.loop(0, high - low)
        def _(it):
            i = high - 1 - it
            qs = pl.ds(pl.multiple_of(i * qb, qb), qb)
            ds = (scores[:, qs] * (dprobs[:, qs] - delta[:, qs])).astype(BF16)
            d_low[:, qs] = ds
            t = dot(kt[...], ds, NN) * (factor[:, qs] * SCALE)
            for b in range(2):
                mine = t[:, b * rows : (b + 1) * rows].T
                zsend[i * 2 + b] = mine.astype(BF16)
                if low == 0 and b == 0:

                    @pl.when(i == 0)
                    def _():
                        dq_own[...] = mine

            for s in range(max(2 * low, 1), 2 * high):

                @pl.when(i == s // 2)
                def _():
                    zc2[s].start()

    key_side(1, probs_low, 8, 2)
    query_side(4, 0)
    key_side(0, d_low, 8, 2)
    key_side(1, probs_low, 2, 0)
    key_side(0, d_low, 2, 0)

    def up(ref):
        return ref.astype(F32)

    yc = {}

    def over_x(part):
        for dy in (1, 0):
            total = pkv[part, dy]
            for slot in range(2, NXY):
                if XY_AT[slot][1] == dy:
                    xc[part, slot].wait_recv()
                    total += up(xrecv[part, slot])
            ysum[part, dy] = total.astype(BF16)
            seq_to, _ = at(dy=dy)
            far = (head + NCORE) % (2 * NCORE)
            if dy:
                yc[part, 0] = remote(
                    ysum.at[part, 1], yrecv.at[part, 0], (seq_to, head)
                )
                yc[part, 0].start()
            yc[part, 1 + dy] = remote(
                ysum.at[part, dy], yrecv.at[part, 1 + dy], (seq_to, far)
            )
            yc[part, 1 + dy].start()

    def columns(out, h):
        return out.at[
            :, pl.ds(pl.multiple_of(h * HEAD_DIM, HEAD_DIM), HEAD_DIM)
        ]

    ends = []
    other = head + 1 - 2 * (head % 2)

    def over_y(part, out):
        yc[part, 0].wait_recv()
        fin[part, 0] = (up(ysum[part, 0]) + up(yrecv[part, 0])).astype(BF16)
        yc[part, 1].wait_recv()
        yc[part, 2].wait_recv()
        fin[part, 1] = (up(yrecv[part, 1]) + up(yrecv[part, 2])).astype(BF16)
        for b in range(2):
            cols = columns(out, (head + NCORE * b) % (2 * NCORE))
            c = remote(fin.at[part, b], cols, (seq, other))
            c.start()
            ends.append(c.wait_recv)
            c = pltpu.make_async_copy(fin.at[part, b], cols, local_sem.at[2 * part + b])
            c.start()
            ends.append(c.wait)

    over_x(1)
    for g in range(len(groups)):
        for d in range(1, NZ):
            stat_copy(g, d).wait_send()
    over_x(0)
    all_sent()
    total = dq_own[...]
    for slot in range(1, NZ):
        zc2[slot].wait_recv()
        total += up(zrecv[slot])
    fin_q[...] = total.astype(BF16)
    cols = columns(oq, head)
    for d in range(1, 2 * NCORE):
        c = remote(fin_q, cols, head_at(d))
        c.start()
        ends.append(c.wait_recv)
    c = pltpu.make_async_copy(fin_q, cols, local_sem.at[4])
    c.start()
    ends.append(c.wait)
    over_y(1, ov)
    over_y(0, ok)
    for wait in ends:
        wait()
    all_sent()


def hand_over(a, b, c, oa, ob, oc):
    oa[...] = a[...]
    ob[...] = b[...]
    oc[...] = c[...]


def local(queries, keys, values, d_out):
    rows, width = queries.shape
    total = NZ * rows
    any_spec = pl.BlockSpec(memory_space=pl.ANY)
    out = jax.ShapeDtypeStruct((rows, 2 * NCORE * width), BF16)
    vm = pltpu.VMEM
    outs = pl.pallas_call(
        kernel,
        out_shape=[out, out, out],
        in_specs=[any_spec] * 4,
        out_specs=[any_spec] * 3,
        scratch_shapes=[
            vm((2, NZ, rows, width), BF16),
            vm((2, NXY, rows, width), BF16),
            vm((total, total), F32),
            vm((total, total), F32),
            vm((total, total), BF16),
            vm((total, total), BF16),
            vm((width, total), BF16),
            vm((2, NZ, rows, width), BF16),
            vm((NZ, 4, 128), F32),
            vm((NZ, NZ, 4, 128), F32),
            vm((1, total), F32),
            vm((1, total), F32),
            vm((1, total), F32),
            vm((2, 2, rows, width), F32),
            vm((rows, width), F32),
            vm((2, NXY, rows, width), BF16),
            vm((2, NXY, rows, width), BF16),
            vm((NZ, rows, width), BF16),
            vm((NZ, rows, width), BF16),
            vm((2, 2, rows, width), BF16),
            vm((2, 3, rows, width), BF16),
            vm((2, 2, rows, width), BF16),
            vm((rows, width), BF16),
            pltpu.SemaphoreType.DMA((5,)),
            pltpu.SemaphoreType.DMA((112,)),
            pltpu.SemaphoreType.DMA((112,)),
        ],
        compiler_params=pltpu.CompilerParams(
            collective_id=0, has_side_effects=True, vmem_limit_bytes=63 * 2**20
        ),
        name="attention_backward",
    )(queries, keys, values, d_out)
    spec = pl.BlockSpec(memory_space=pltpu.VMEM)
    return pl.pallas_call(
        hand_over,
        out_shape=[out, out, out],
        in_specs=[spec] * 3,
        out_specs=[spec] * 3,
        name="hand_over",
    )(*outs)


def solution(mesh):
    in_specs = (P("seq", "head"), P("seq", "head"), P("seq", "head"), P("seq", "head"))
    out_specs = (P("seq", None), P("seq", None), P("seq", None))
    return jax.shard_map(local, mesh=mesh, in_specs=in_specs, out_specs=out_specs, check_vma=False)
```

```python
import math

import jax
import jax.numpy as jnp
from jax import lax
from jax.experimental import pallas as pl
from jax.experimental.pallas import tpu as pltpu
from jax.sharding import PartitionSpec as P

HEAD_DIM = 128
NZ, NX, NY = 8, 4, 2
NXY = NX * NY
NCORE = 2
SCALE = 1.0 / math.sqrt(HEAD_DIM)
LOG2E_SCALE = math.log2(math.e) * SCALE
MESH = pl.DeviceIdType.MESH
F32 = jnp.float32
BF16 = jnp.bfloat16
NT = (((1,), (1,)), ((), ()))
NN = (((1,), (0,)), ((), ()))


def dot(a, b, dims):
    return lax.dot_general(a, b, dims, preferred_element_type=F32)


Z_AT = [0, 1, -1, 2, -2, 3, -3, 4]
XY_AT = [(0, 0), (0, 1), (1, 0), (-1, 0), (2, 0), (1, 1), (-1, 1), (2, 1)]


def kernel(
    q_in,
    k_in,
    v_in,
    do_in,
    oq,
    ok,
    ov,
    qd,
    kv,
    scores,
    dprobs,
    probs_low,
    d_low,
    kt,
    qdf,
    st_own,
    st_all,
    lse,
    delta,
    factor,
    pkv,
    dq_own,
    xsend,
    xrecv,
    zsend,
    zrecv,
    ysum,
    yrecv,
    fin,
    fin_q,
    local_sem,
    send_sem,
    recv_sem,
):
    rows = q_in.shape[0]
    total_q = NZ * rows
    total_k = NXY * rows
    seq = lax.axis_index("seq")
    head = lax.axis_index("head")
    z = seq // NXY
    x = (seq // NY) % NX
    y = seq % NY

    def at(dz=0, dx=0, dy=0):
        zz = (z + dz + NZ) % NZ
        xx = (x + dx + NX) % NX
        yy = (y + dy) % NY
        return (zz * NXY + xx * NY + yy, head)

    def head_at(dh):
        return (seq, (head + dh) % (2 * NCORE))

    counter = [0]
    sent = []

    def remote(src, dst, device):
        i = counter[0]
        counter[0] += 1
        c = pltpu.make_async_remote_copy(
            src_ref=src,
            dst_ref=dst,
            send_sem=send_sem.at[i],
            recv_sem=recv_sem.at[i],
            device_id=device,
            device_id_type=MESH,
        )
        sent.append(c)
        return c

    def all_sent():
        while sent:
            sent.pop().wait_send()

    own = [
        pltpu.make_async_copy(src, dst, local_sem.at[i])
        for i, (src, dst) in enumerate(
            [
                (q_in, qd.at[0, 0]),
                (do_in, qd.at[1, 0]),
                (k_in, kv.at[0, 0]),
                (v_in, kv.at[1, 0]),
            ]
        )
    ]
    for c in own:
        c.start()

    barrier = pltpu.get_barrier_semaphore()
    peers = [at(dz=1), at(dz=-1), at(dx=1), at(dx=-1), at(dx=2), at(dy=1)]
    peers += [head_at(d) for d in range(1, 2 * NCORE)]
    for p in peers:
        pl.semaphore_signal(barrier, inc=1, device_id=p, device_id_type=MESH)
    for c in own:
        c.wait()
    pl.semaphore_wait(barrier, len(peers))

    qb = 2 * rows
    nq = NZ // 2
    half = rows // 2
    zc, kc = {}, {}

    def z_send(a, b, part, h, dz):
        rs = pl.ds(h * half, half)
        c = remote(qd.at[part, a, rs], qd.at[part, b, rs], at(dz=dz))
        zc[b, part, h] = c
        c.start()

    def z_round(a, part, h):
        zc[a, part, h].wait_recv()
        z_send(a, a + 2, part, h, 1)
        zc[a - 1, part, h].wait_recv()
        z_send(a - 1, a + 1, part, h, -1)
        if a == 4:
            if part == 0:
                z_send(4, 7, part, h, 2)
            else:
                z_send(3, 7, part, h, -2)

    def k_send(a, b, part, device):
        c = remote(kv.at[part, a], kv.at[part, b], device)
        kc[b, part] = c
        c.start()

    for part in range(2):
        for h in range(2):
            z_send(0, 2, part, h, 1)
            z_send(0, 1, part, h, -1)
        k_send(0, 1, part, at(dy=1))
        k_send(0, 3, part, at(dx=1))
        k_send(0, 2, part, at(dx=-1))
    for part in range(2):
        k_send(0, 4, part, at(dx=2))

    groups = ((0, 5), (5, 2), (7, 1))
    st_base = counter[0]
    counter[0] += len(groups) * (NZ - 1)

    def stat_copy(g, d):
        k = st_base + g * (NZ - 1) + d - 1
        slots = pl.ds(*groups[g])
        return pltpu.make_async_remote_copy(
            src_ref=st_own.at[slots],
            dst_ref=st_all.at[d, slots],
            send_sem=send_sem.at[k],
            recv_sem=recv_sem.at[k],
            device_id=at(dz=d),
            device_id_type=MESH,
        )

    def block(c0, cn, k0, kn):
        first, last = k0 == 0, k0 + kn == NXY
        qs = pl.ds(c0 * rows, cn * rows)
        ks = pl.ds(k0 * rows, kn * rows)
        slots = pl.ds(c0, cn)
        qq = qd[0, slots].reshape(cn * rows, HEAD_DIM)
        dd = qd[1, slots].reshape(cn * rows, HEAD_DIM)
        s = dot(kv[0, pl.ds(k0, kn)].reshape(kn * rows, HEAD_DIM), qq, NT)
        scores[ks, qs] = s
        m = jnp.max(s, axis=0, keepdims=True) * LOG2E_SCALE
        if not first:
            old = lse[:, qs]
            m = jnp.maximum(m, old)
        e = jnp.exp2(s * LOG2E_SCALE - m)
        dp = dot(kv[1, pl.ds(k0, kn)].reshape(kn * rows, HEAD_DIM), dd, NT)
        dprobs[ks, qs] = dp
        l = jnp.sum(e, axis=0, keepdims=True)
        w = jnp.sum(e * dp, axis=0, keepdims=True)
        if not first:
            fade = jnp.exp2(old - m)
            l += fade * factor[:, qs]
            w += fade * delta[:, qs]
        if last:
            m = m + jnp.log2(l)
            w = w / l
            for c in range(cn):
                for r in range(2):
                    lanes = slice((2 * c + r) * 128, (2 * c + r + 1) * 128)
                    st_own[c0 + c, pl.ds(r, 1), :] = m[:, lanes]
                    st_own[c0 + c, pl.ds(2 + r, 1), :] = w[:, lanes]
        else:
            factor[:, qs] = l
            delta[:, qs] = w
        lse[:, qs] = m

    def spread(part):
        kc[1, part].wait_recv()
        k_send(1, 6, part, at(dx=1))
        k_send(1, 5, part, at(dx=-1))

    def far_keys(part):
        kc[4, part].wait_recv()
        k_send(4, 7, part, at(dy=1))

    z_round(2, 0, 0)
    z_round(2, 0, 1)
    z_round(2, 1, 0)
    spread(0)
    z_round(2, 1, 1)
    spread(1)
    for part in range(2):
        kc[2, part].wait_recv()
        kc[3, part].wait_recv()
    z_round(4, 0, 0)
    z_round(4, 0, 1)
    far_keys(0)
    z_round(4, 1, 0)
    z_round(4, 1, 1)
    far_keys(1)
    block(0, 3, 0, 4)
    block(3, 2, 0, 4)
    for part in range(2):
        kc[5, part].wait_recv()
        kc[6, part].wait_recv()
    block(0, 3, 4, 3)
    block(3, 2, 4, 3)
    kc[7, 0].wait_recv()
    kc[7, 1].wait_recv()
    block(0, 5, 7, 1)
    for part in range(2):
        for h in range(2):
            zc[6, part, h].wait_recv()
            zc[5, part, h].wait_recv()
    for d in (1, 7, 2, 6, 3, 5):
        stat_copy(0, d).start()
    block(5, 2, 0, NXY)
    for part in range(2):
        for h in range(2):
            zc[7, part, h].wait_recv()
    stat_copy(0, 4).start()
    for d in (4, 3, 5, 2, 6, 1, 7):
        stat_copy(1, d).start()
    block(7, 1, 0, NXY)
    for d in (4, 3, 5, 2, 6, 1, 7):
        stat_copy(2, d).start()

    for j in range(NXY):
        kt[:, pl.ds(j * rows, rows)] = kv[0, j].T

    @pl.loop(0, NXY)
    def _(j):
        ks = pl.ds(pl.multiple_of(j * rows, rows), rows)
        p = jnp.exp2(scores[ks, :] * LOG2E_SCALE - lse[...])
        scores[ks, :] = p
        probs_low[ks, :] = p.astype(BF16)

    all_sent()

    st_all[0] = st_own[...]
    for g in range(len(groups)):
        for d in range(1, NZ):
            stat_copy(g, d).wait_recv()
    for slot, dz in enumerate(Z_AT):
        tops, deltas = [], []
        for d in range(NZ):
            there = Z_AT.index((dz + d + 3) % NZ - 3)
            tops.append(st_all[d, there, pl.ds(0, 2), :])
            deltas.append(st_all[d, there, pl.ds(2, 2), :])
        big = tops[0]
        for t in tops[1:]:
            big = jnp.maximum(big, t)
        mass = jnp.zeros_like(big)
        weighted = jnp.zeros_like(big)
        for t, w in zip(tops, deltas):
            f = jnp.exp2(t - big)
            mass += f
            weighted += f * w
        weighted = weighted / mass
        own_factor = jnp.exp2(tops[0] - (big + jnp.log2(mass)))
        for r in range(2):
            cols = pl.ds(slot * rows + r * 128, 128)
            delta[:, cols] = weighted[r : r + 1, :]
            factor[:, cols] = own_factor[r : r + 1, :]
        wide = jnp.broadcast_to(
            factor[:, pl.ds(slot * rows, rows)], (HEAD_DIM, rows)
        ).T
        for part in range(2):
            qdf[part, slot] = (qd[part, slot].astype(F32) * wide).astype(BF16)

    xc = {}
    for part in (1, 0):
        for slot in range(2, NXY):
            dx, dy = XY_AT[slot]
            xc[part, slot] = remote(
                xsend.at[part, slot], xrecv.at[part, slot], at(dx=dx)
            )
    zc2 = {
        slot: remote(zsend.at[slot], zrecv.at[slot], at(dz=Z_AT[slot]))
        for slot in range(1, NZ)
    }

    def key_side(part, left, high, low):
        @pl.loop(0, (high - low) // 2)
        def _(it):
            slot = high - 2 - 2 * it
            ks = pl.ds(pl.multiple_of(slot * rows, rows), 2 * rows)
            t = dot(left[ks, :], qdf[part].reshape(total_q, HEAD_DIM), NN)
            if part == 0:
                t = t * SCALE
            t = t.reshape(2, rows, HEAD_DIM)
            if low == 0:

                @pl.when(slot == 0)
                def _():
                    pkv[part] = t

            xsend[part, pl.ds(slot, 2)] = t.astype(BF16)
            for s in range(max(low, 2), high, 2):

                @pl.when(slot == s)
                def _():
                    xc[part, s + 1].start()
                    xc[part, s].start()

    def query_side(high, low):
        @pl.loop(0, high - low)
        def _(it):
            i = high - 1 - it
            qs = pl.ds(pl.multiple_of(i * qb, qb), qb)
            ds = (scores[:, qs] * (dprobs[:, qs] - delta[:, qs])).astype(BF16)
            d_low[:, qs] = ds
            t = dot(kt[...], ds, NN) * (factor[:, qs] * SCALE)
            for b in range(2):
                mine = t[:, b * rows : (b + 1) * rows].T
                zsend[i * 2 + b] = mine.astype(BF16)
                if low == 0 and b == 0:

                    @pl.when(i == 0)
                    def _():
                        dq_own[...] = mine

            for s in range(max(2 * low, 1), 2 * high):

                @pl.when(i == s // 2)
                def _():
                    zc2[s].start()

    for slot in (7, 6):
        t = dot(
            probs_low[pl.ds(slot * rows, rows), :],
            qdf[1].reshape(total_q, HEAD_DIM),
            NN,
        )
        xsend[1, slot] = t.astype(BF16)
        xc[1, slot].start()
    key_side(1, probs_low, 6, 2)
    query_side(4, 0)
    key_side(0, d_low, 8, 2)
    key_side(1, probs_low, 2, 0)
    key_side(0, d_low, 2, 0)

    def up(ref):
        return ref.astype(F32)

    yc = {}

    def over_x(part):
        for dy in (1, 0):
            total = pkv[part, dy]
            for slot in range(2, NXY):
                if XY_AT[slot][1] == dy:
                    xc[part, slot].wait_recv()
                    total += up(xrecv[part, slot])
            ysum[part, dy] = total.astype(BF16)
            seq_to, _ = at(dy=dy)
            far = (head + NCORE) % (2 * NCORE)
            if dy:
                yc[part, 0] = remote(
                    ysum.at[part, 1], yrecv.at[part, 0], (seq_to, head)
                )
                yc[part, 0].start()
            yc[part, 1 + dy] = remote(
                ysum.at[part, dy], yrecv.at[part, 1 + dy], (seq_to, far)
            )
            yc[part, 1 + dy].start()

    def columns(out, h):
        return out.at[
            :, pl.ds(pl.multiple_of(h * HEAD_DIM, HEAD_DIM), HEAD_DIM)
        ]

    ends = []
    other = head + 1 - 2 * (head % 2)

    def over_y(part, out):
        yc[part, 0].wait_recv()
        fin[part, 0] = (up(ysum[part, 0]) + up(yrecv[part, 0])).astype(BF16)
        yc[part, 1].wait_recv()
        yc[part, 2].wait_recv()
        fin[part, 1] = (up(yrecv[part, 1]) + up(yrecv[part, 2])).astype(BF16)
        for b in range(2):
            cols = columns(out, (head + NCORE * b) % (2 * NCORE))
            c = remote(fin.at[part, b], cols, (seq, other))
            c.start()
            ends.append(c.wait_recv)
            c = pltpu.make_async_copy(fin.at[part, b], cols, local_sem.at[2 * part + b])
            c.start()
            ends.append(c.wait)

    over_x(1)
    for g in range(len(groups)):
        for d in range(1, NZ):
            stat_copy(g, d).wait_send()
    over_x(0)
    all_sent()
    total = dq_own[...]
    for slot in range(1, NZ):
        zc2[slot].wait_recv()
        total += up(zrecv[slot])
    fin_q[...] = total.astype(BF16)
    cols = columns(oq, head)
    for d in range(1, 2 * NCORE):
        c = remote(fin_q, cols, head_at(d))
        c.start()
        ends.append(c.wait_recv)
    c = pltpu.make_async_copy(fin_q, cols, local_sem.at[4])
    c.start()
    ends.append(c.wait)
    over_y(1, ov)
    over_y(0, ok)
    for wait in ends:
        wait()
    all_sent()


def hand_over(a, b, c, oa, ob, oc):
    oa[...] = a[...]
    ob[...] = b[...]
    oc[...] = c[...]


def local(queries, keys, values, d_out):
    rows, width = queries.shape
    total = NZ * rows
    any_spec = pl.BlockSpec(memory_space=pl.ANY)
    out = jax.ShapeDtypeStruct((rows, 2 * NCORE * width), BF16)
    vm = pltpu.VMEM
    outs = pl.pallas_call(
        kernel,
        out_shape=[out, out, out],
        in_specs=[any_spec] * 4,
        out_specs=[any_spec] * 3,
        scratch_shapes=[
            vm((2, NZ, rows, width), BF16),
            vm((2, NXY, rows, width), BF16),
            vm((total, total), F32),
            vm((total, total), F32),
            vm((total, total), BF16),
            vm((total, total), BF16),
            vm((width, total), BF16),
            vm((2, NZ, rows, width), BF16),
            vm((NZ, 4, 128), F32),
            vm((NZ, NZ, 4, 128), F32),
            vm((1, total), F32),
            vm((1, total), F32),
            vm((1, total), F32),
            vm((2, 2, rows, width), F32),
            vm((rows, width), F32),
            vm((2, NXY, rows, width), BF16),
            vm((2, NXY, rows, width), BF16),
            vm((NZ, rows, width), BF16),
            vm((NZ, rows, width), BF16),
            vm((2, 2, rows, width), BF16),
            vm((2, 3, rows, width), BF16),
            vm((2, 2, rows, width), BF16),
            vm((rows, width), BF16),
            pltpu.SemaphoreType.DMA((5,)),
            pltpu.SemaphoreType.DMA((112,)),
            pltpu.SemaphoreType.DMA((112,)),
        ],
        compiler_params=pltpu.CompilerParams(
            collective_id=0, has_side_effects=True, vmem_limit_bytes=63 * 2**20
        ),
        name="attention_backward",
    )(queries, keys, values, d_out)
    spec = pl.BlockSpec(memory_space=pltpu.VMEM)
    return pl.pallas_call(
        hand_over,
        out_shape=[out, out, out],
        in_specs=[spec] * 3,
        out_specs=[spec] * 3,
        name="hand_over",
    )(*outs)


def solution(mesh):
    in_specs = (P("seq", "head"), P("seq", "head"), P("seq", "head"), P("seq", "head"))
    out_specs = (P("seq", None), P("seq", None), P("seq", None))
    return jax.shard_map(local, mesh=mesh, in_specs=in_specs, out_specs=out_specs, check_vma=False)
```
